512 devices in a mesh: dp: 8 (over z_hi, y), vocab: 64 (over z_lo, x, core).
Axes of the slice: x: 4, y: 4, z: 16 (z_hi: 2, z_lo: 8; z = z_hi * 8 + z_lo), core: 2. Of those that a mesh axis runs over, the one named last changes fastest.
Arguments:
- hidden: bfloat16 [1024, 5120], P('dp', 'vocab'), may hold values from -8 to 8
- head_weight: bfloat16 [5120, 76032], P('dp', 'vocab'), may hold values from -0.25 to 0.25
- teacher_logits: bfloat16 [1024, 76032], P(('dp', 'vocab')), may hold values from -30 to 330
- block_owner: int32 [64], replicated, may hold values from 0 to 63, each once
- sampled_ids: int32 [1024], P('dp'), may hold values from 0 to 76031
- loss_weight: float32 [1024], P('dp'), may hold values from 1 to 10
Outputs:
- grad_hidden: float32 [1024, 5120], P('dp', 'vocab')
- divergence: float32 [1024], P('dp')
- sampled_logp: float32 [1024], P('dp')
The draws below stay inside these ranges and needn't reach their ends.
Inputs may be any that keep to these rules, and one draw needn't show every extreme that they name: `block_owner`: each of the 64 numbers appears once.
All inputs are finite; a program needn't handle non-finite values.
Results may differ from the reference program's by a relative error of at most 0.003.
Values may be sent and summed in bfloat16 or wider, within the bound.
A program may use at most 64 MiB of HBM per device.

```python
import math
import jax
import jax.numpy as jnp

D = 5120
VOCAB = 76032
TOKENS = 1024
BLOCKS = 64


def draw_head_weight(key, part):
    key = jax.random.fold_in(key, 1)
    column = jnp.arange(VOCAB, dtype=jnp.float32)
    col_scale = 3.0 * D ** (-0.5) * (0.85 + 0.15 * column / (VOCAB - 1))
    values = jnp.clip(jax.random.normal(key, (D, VOCAB), jnp.float32), -5.0, 5.0) * col_scale[None, :]
    return jnp.clip(values, -0.25, 0.25).astype(jnp.bfloat16)


def draw_hidden(key, part):
    key = jax.random.fold_in(key, 2)
    scale_key, value_key = jax.random.split(key)
    row_scale = jnp.exp(jax.random.uniform(scale_key, (TOKENS, 1), jnp.float32, jnp.log(0.5), jnp.log(2.0)))
    values = jnp.clip(jax.random.normal(value_key, (TOKENS, D), jnp.float32), -4.0, 4.0) * row_scale
    return values.astype(jnp.bfloat16)


def draw_teacher_logits(key, part):
    key = jax.random.fold_in(key, 3)
    scale_key, value_key = jax.random.split(key)
    row_scale = 3.5 * jnp.exp(jax.random.uniform(scale_key, (TOKENS, 1), jnp.float32, jnp.log(0.7), jnp.log(1.4)))
    values = jnp.clip(jax.random.normal(value_key, (TOKENS, VOCAB), jnp.float32), -6.0, 6.0) * row_scale
    return values.astype(jnp.bfloat16)


def place_ends(drawn, stream_key, low, high):
    longest = drawn.shape.index(max(drawn.shape))
    spots = []
    for shift in (0, 1):
        where = [jax.random.randint(jax.random.fold_in(stream_key, axis), (), 0, length) for axis, length in enumerate(drawn.shape)]
        where[longest] = (where[longest] + shift) % drawn.shape[longest]
        spots.append(tuple(where))
    return drawn.at[spots[0]].set(low).at[spots[1]].set(high)


def levels(own_key, extent, shards, smallest, top_value):
    gain, own = 1.0, jax.random.fold_in(own_key, 6)
    for axis_at, shards_of in shards:
        heights = jnp.exp(jax.random.uniform(jax.random.fold_in(own, axis_at), (shards_of,), jnp.float32, smallest / len(shards), top_value / len(shards)))
        gain = gain * jnp.repeat(heights, extent[axis_at] // shards_of).reshape([-1 if axis == axis_at else 1 for axis in range(len(extent))])
    return gain


def setup_inputs(seed: int = 0) -> dict:
    splits = jax.random.split(jax.random.key(seed), 7)
    hidden = draw_hidden(jax.random.fold_in(splits[6], 71), 0)
    head_weight = draw_head_weight(jax.random.fold_in(splits[6], 71), 0)
    teacher_logits = draw_teacher_logits(jax.random.fold_in(splits[6], 71), 0)
    block_owner = jax.random.permutation(splits[3], BLOCKS).astype(jnp.int32)
    sampled_ids = place_ends(jax.random.randint(splits[4], (TOKENS,), 0, VOCAB), jax.random.fold_in(splits[4], 1), 0, VOCAB - 1).astype(jnp.int32)
    loss_weight = jnp.clip(jnp.exp(math.log(10.0) - 2.3025851 * jax.random.uniform(splits[5], (TOKENS,), jnp.float32) ** levels(splits[5], (TOKENS,), ((0, 8),), -0.2, 0.2)), 1.0, 10.0)
    return {"hidden": hidden, "head_weight": head_weight, "teacher_logits": teacher_logits, "block_owner": block_owner, "sampled_ids": sampled_ids, "loss_weight": loss_weight}


def reference(hidden, head_weight, teacher_logits, block_owner, sampled_ids, loss_weight):
    teacher_blocks = teacher_logits.reshape(TOKENS, BLOCKS, VOCAB // BLOCKS)
    teacher = jnp.zeros_like(teacher_blocks).at[:, block_owner].set(teacher_blocks)
    teacher = teacher.reshape(TOKENS, VOCAB).astype(jnp.float32)
    logits = jnp.dot(hidden, head_weight, preferred_element_type=jnp.float32)
    student_top = jnp.max(logits, axis=1, keepdims=True)
    student_exp = jnp.exp(logits - student_top)
    student_sum = jnp.sum(student_exp, axis=1, keepdims=True)
    student_lse = student_top + jnp.log(student_sum)
    teacher_top = jnp.max(teacher, axis=1, keepdims=True)
    teacher_lse = teacher_top + jnp.log(jnp.sum(jnp.exp(teacher - teacher_top), axis=1, keepdims=True))
    gap_logits = logits - teacher
    divergence = jnp.sum(student_exp * gap_logits, axis=1, keepdims=True) / student_sum - student_lse + teacher_lse
    picked = jnp.take_along_axis(logits, sampled_ids.astype(jnp.int32)[:, None], axis=1)
    sampled_logp = picked - student_lse
    student_prob = jnp.exp(logits - student_lse)
    grad_logits = (loss_weight[:, None] * student_prob * (gap_logits - student_lse + teacher_lse - divergence)).astype(jnp.bfloat16)
    grad_hidden = jnp.dot(grad_logits, head_weight.T, preferred_element_type=jnp.float32)
    return grad_hidden, divergence[:, 0], sampled_logp[:, 0]
```

```python
import jax
import jax.numpy as jnp
from jax import lax
from jax.experimental import pallas as pl
from jax.experimental.pallas import tpu as pltpu
from jax.sharding import PartitionSpec as P

MESH = pl.DeviceIdType.MESH
F32 = jnp.float32
BF16 = jnp.bfloat16

VD = 1188
VC = 256
NC = 5
VP = VC * NC
KS = 640
KH = 4 * KS
TK = 128
OB = 80


def kernel(
    inv_ref, hid_ref, w_ref, tea_ref, ids_ref, lw_ref,
    out_ref, tok_ref,
    Hb, hh, Wc, Sb, Rb, L, Fp, TP, TQ, F2, TR, TT,
    St, StA, St2, StB, Zt, GL, GT, RC, X1, RX, X2, RZ,
    s1s, s1r, s2s, s2r, s3s, s3r, ws, wr, zs_, zr_,
    tas, tar, tbs, tbr, sas, sar, sbs, sbr, gs, gr, cs, cr, xs, xr, rzs, rzr,
):
    dp = lax.axis_index("dp")
    v = lax.axis_index("vocab")
    h = lax.div(dp, 4)
    q = lax.rem(dp, 4)
    zl = lax.div(v, 8)
    e = lax.rem(v, 8)
    x = lax.div(e, 2)
    c = lax.rem(e, 2)
    z = h * 8 + zl
    oh = 1 - h
    hb = lax.div(zl, 4)
    ip = lax.rem(zl, 4)

    def at_z(zz):
        return (lax.div(zz, 8) * 4 + q, lax.rem(zz, 8) * 8 + e)

    def at_y(yy):
        return (h * 4 + yy, v)

    def at_e(ee):
        return (dp, zl * 8 + ee)

    partner = at_z(oh * 8 + zl)
    sibling = at_e(x * 2 + 1 - c)

    def copy(src, dst, ss, rs, dev):
        return pltpu.make_async_remote_copy(
            src_ref=src, dst_ref=dst, send_sem=ss, recv_sem=rs, device_id=dev, device_id_type=MESH
        )

    barrier = pltpu.get_barrier_semaphore()

    def greet_z(k, _):
        pl.semaphore_signal(barrier, inc=1, device_id=at_z(lax.rem(z + k, 16)), device_id_type=MESH)
        return _

    def greet_y(k, _):
        pl.semaphore_signal(barrier, inc=1, device_id=at_y(lax.rem(q + k, 4)), device_id_type=MESH)
        return _

    def greet_e(k, _):
        pl.semaphore_signal(barrier, inc=1, device_id=at_e(lax.rem(e + k, 8)), device_id_type=MESH)
        return _

    lax.fori_loop(1, 16, greet_z, 0)
    lax.fori_loop(1, 4, greet_y, 0)
    lax.fori_loop(1, 8, greet_e, 0)

    wrow = pl.multiple_of(q * KS, KS)
    for k in range(NC - 1):
        Wc[k, pl.ds(wrow, KS), :] = w_ref[:, k * VC:(k + 1) * VC]
    tail = VD - (NC - 1) * VC
    Wc[NC - 1, pl.ds(wrow, KS), :] = jnp.zeros((KS, VC), BF16)
    Wc[NC - 1, pl.ds(wrow, KS), 0:tail] = w_ref[:, (NC - 1) * VC:VD]

    pl.semaphore_wait(barrier, 25)

    def feat_copy(k):
        return copy(hid_ref, Hb.at[h, ip, x, c], s1s.at[k], s1r.at[h * 4 + ip], at_z(hb * 8 + k))

    def s1_send(k, _):
        @pl.when(hb * 8 + k != z)
        def _go():
            feat_copy(k).start()
        return _

    lax.fori_loop(0, 8, s1_send, 0)

    @pl.when(hb == h)
    def _own():
        Hb[h, ip, x, c] = hid_ref[...]

    def w_copy(ch, k):
        sl = Wc.at[ch, pl.ds(wrow, KS)]
        return copy(sl, sl, ws.at[ch * 3 + k - 1], wr.at[ch * 3 + k - 1], at_y(lax.rem(q + k, 4)))

    def w_send(ch):
        for k in (1, 3, 2):
            w_copy(ch, k).start()

    def w_wait_recv(ch):
        for k in (1, 2, 3):
            sl = Wc.at[ch, pl.ds(pl.multiple_of(lax.rem(q + 4 - k, 4) * KS, KS), KS)]
            copy(sl, sl, ws.at[ch * 3 + k - 1], wr.at[ch * 3 + k - 1], at_y(lax.rem(q + k, 4))).wait_recv()

    w_send(0)
    w_send(1)

    def pack(zz, _):
        for d in range(8):
            Fp[2 * d:2 * d + 2, :] = tea_ref[inv_ref[zz * 8 + d]]
        TP[zz] = Fp[...].astype(BF16)
        return _

    lax.fori_loop(0, 8, pack, 0)

    def ta_copy(k):
        to = lax.rem(zl + k, 8)
        return copy(TP.at[to], TQ.at[zl], tas.at[k - 1], tar.at[k - 1], at_z(h * 8 + to))

    def ta_send(k, _):
        ta_copy(k).start()
        return _

    lax.fori_loop(1, 8, ta_send, 0)
    TQ[zl] = TP[zl]

    def s2_copy(g, k):
        sl = Hb.at[g, :, x, c]
        return copy(sl, sl, s2s.at[g * 3 + k - 1], s2r.at[g * 3 + k - 1],
                    at_e(lax.rem(x + k, 4) * 2 + c))

    def s2_from(g, k):
        sl = Hb.at[g, :, lax.rem(x + 4 - k, 4), c]
        return copy(sl, sl, s2s.at[g * 3 + k - 1], s2r.at[g * 3 + k - 1],
                    at_e(lax.rem(x + k, 4) * 2 + c))

    def s3_copy(g):
        sl = Hb.at[g, :, :, c]
        return copy(sl, sl, s3s.at[g], s3r.at[g], sibling)

    def s3_from(g):
        sl = Hb.at[g, :, :, 1 - c]
        return copy(sl, sl, s3s.at[g], s3r.at[g], sibling)

    for g in (oh, h):
        def s1_wait(i, _):
            src = g * 8 + h * 4 + i

            @pl.when(src != z)
            def _go():
                sl = Hb.at[g, i, x, c]
                copy(hid_ref, sl, s1s.at[0], s1r.at[g * 4 + i], partner).wait_recv()
            return _

        lax.fori_loop(0, 4, s1_wait, 0)
        for k in (1, 3, 2):
            s2_copy(g, k).start()

    for g in (oh, h):
        for k in (1, 2, 3):
            s2_from(g, k).wait_recv()
        s3_copy(g).start()

    for g in (oh, h):
        s3_from(g).wait_recv()
        for i in range(4):
            blk = Hb[g, i].reshape(KS, TK)
            hh[g, :, i * KS:(i + 1) * KS] = blk.T

    def z_copy(ch):
        return copy(Sb.at[ch], Rb.at[ch], zs_.at[ch], zr_.at[ch], partner)

    def chunk(ch, _):
        w_wait_recv(ch)

        @pl.when(ch + 2 < NC)
        def _next():
            w_send(ch + 2)

        Sb[ch] = jnp.dot(hh[oh], Wc[ch], preferred_element_type=F32)
        z_copy(ch).start()
        L[ch] = jnp.dot(hh[h], Wc[ch], preferred_element_type=F32)
        return _

    lax.fori_loop(0, NC, chunk, 0)

    def ta_wait(k, _):
        frm = lax.rem(zl + 8 - k, 8)
        copy(TP.at[0], TQ.at[frm], tas.at[k - 1], tar.at[k - 1], partner).wait_recv()
        return _

    lax.fori_loop(1, 8, ta_wait, 0)
    for zz in range(8):
        rows = TQ[zz].astype(F32)
        for d in range(8):
            F2[d, 2 * zz:2 * zz + 2, :] = rows[2 * d:2 * d + 2]

    def tr_cast(d, _):
        TR[d] = F2[d].astype(BF16)
        return _

    lax.fori_loop(0, 8, tr_cast, 0)

    def tb_copy(k):
        to = lax.rem(e + k, 8)
        return copy(TR.at[to], TT.at[e], tbs.at[k - 1], tbr.at[k - 1], at_e(to))

    def tb_send(k, _):
        tb_copy(k).start()
        return _

    lax.fori_loop(1, 8, tb_send, 0)
    TT[e] = TR[e]

    def tb_wait(k, _):
        frm = lax.rem(e + 8 - k, 8)
        copy(TR.at[0], TT.at[frm], tbs.at[k - 1], tbr.at[k - 1], sibling).wait_recv()
        return _

    lax.fori_loop(1, 8, tb_wait, 0)

    lane = lax.broadcasted_iota(jnp.int32, (TK, VC), 1)
    low = F32(-3.0e38)

    def tea(ch):
        return TT[:, :, ch * VC:(ch + 1) * VC].reshape(TK, VC).astype(F32)

    m_s = jnp.full((TK, 1), low, F32)
    m_t = jnp.full((TK, 1), low, F32)
    for ch in range(NC):
        z_copy(ch).wait_recv()
        val = L[ch] + Rb[ch]
        L[ch] = val
        t = tea(ch)
        if ch == NC - 1:
            val = jnp.where(lane < tail, val, low)
            t = jnp.where(lane < tail, t, low)
        m_s = jnp.maximum(m_s, jnp.max(val, axis=1, keepdims=True))
        m_t = jnp.maximum(m_t, jnp.max(t, axis=1, keepdims=True))

    s_sum = jnp.zeros((TK, 1), F32)
    s_gap = jnp.zeros((TK, 1), F32)
    s_pick = jnp.zeros((TK, 1), F32)
    s_tea = jnp.zeros((TK, 1), F32)
    here = ids_ref[...] - v * VD
    for ch in range(NC):
        val = L[ch]
        t = tea(ch)
        ex = jnp.exp(val - m_s)
        et = jnp.exp(t - m_t)
        eg = ex * (val - t)
        pk = jnp.where(lane + ch * VC == here, val, 0.0)
        if ch == NC - 1:
            ok = lane < tail
            ex = jnp.where(ok, ex, 0.0)
            et = jnp.where(ok, et, 0.0)
            eg = jnp.where(ok, eg, 0.0)
            pk = jnp.where(ok, pk, 0.0)
        s_sum = s_sum + jnp.sum(ex, axis=1, keepdims=True)
        s_gap = s_gap + jnp.sum(eg, axis=1, keepdims=True)
        s_pick = s_pick + jnp.sum(pk, axis=1, keepdims=True)
        s_tea = s_tea + jnp.sum(et, axis=1, keepdims=True)

    sl = lax.broadcasted_iota(jnp.int32, (TK, 128), 1)
    pack_cols = jnp.zeros((TK, 128), F32)
    for n, col in enumerate((m_s, s_sum, s_gap, s_pick, m_t, s_tea)):
        pack_cols = jnp.where(sl == n, col, pack_cols)
    St[...] = pack_cols.T[0:8]

    def combine(ref):
        ms = ref[0, 0:1]
        mt = ref[0, 4:5]
        for j in range(1, 8):
            ms = jnp.maximum(ms, ref[j, 0:1])
            mt = jnp.maximum(mt, ref[j, 4:5])
        a = b = p = t = jnp.zeros((1, TK), F32)
        for j in range(8):
            f = jnp.exp(ref[j, 0:1] - ms)
            a = a + ref[j, 1:2] * f
            b = b + ref[j, 2:3] * f
            p = p + ref[j, 3:4]
            t = t + ref[j, 5:6] * jnp.exp(ref[j, 4:5] - mt)
        return ms, a, b, p, mt, t

    def sa_copy(k):
        return copy(St, StA.at[e], sas.at[k - 1], sar.at[k - 1], at_e(lax.rem(e + k, 8)))

    def sa_send(k, _):
        sa_copy(k).start()
        return _

    def sa_wait(k, _):
        copy(St, StA.at[lax.rem(e + 8 - k, 8)], sas.at[k - 1], sar.at[k - 1], sibling).wait_recv()
        return _

    lax.fori_loop(1, 8, sa_send, 0)
    StA[e] = St[...]
    lax.fori_loop(1, 8, sa_wait, 0)
    row = lax.broadcasted_iota(jnp.int32, (8, TK), 0)
    acc = jnp.zeros((8, TK), F32)
    for n, val in enumerate(combine(StA)):
        acc = jnp.where(row == n, val, acc)
    St2[...] = acc

    def sb_copy(k):
        return copy(St2, StB.at[zl], sbs.at[k - 1], sbr.at[k - 1], at_z(h * 8 + lax.rem(zl + k, 8)))

    def sb_send(k, _):
        sb_copy(k).start()
        return _

    def sb_wait(k, _):
        copy(St2, StB.at[lax.rem(zl + 8 - k, 8)], sbs.at[k - 1], sbr.at[k - 1], sibling).wait_recv()
        return _

    lax.fori_loop(1, 8, sb_send, 0)
    StB[zl] = St2[...]
    lax.fori_loop(1, 8, sb_wait, 0)
    ms, a, b, p, mt, t = combine(StB)
    s_lse = ms + jnp.log(a)
    t_lse = mt + jnp.log(t)
    div = b / a - s_lse + t_lse
    tok = jnp.zeros((8, TK), F32)
    for n, val in enumerate((div, p - s_lse, s_lse, t_lse)):
        tok = jnp.where(row == n, val, tok)
    tok_ref[...] = tok
    Zt[...] = jnp.zeros((128, TK), F32)
    Zt[0:8, :] = tok
    cols = Zt[...].T
    c_div = cols[:, 0:1]
    c_s = cols[:, 2:3]
    c_t = cols[:, 3:4]
    lw = lw_ref[...]

    def g_copy(ch):
        sl = GL.at[h, ch]
        return copy(sl, sl, gs.at[ch], gr.at[ch], partner)

    for ch in range(NC):
        val = L[ch]
        gl = lw * jnp.exp(val - c_s) * ((val - tea(ch)) - c_s + c_t - c_div)
        if ch == NC - 1:
            gl = jnp.where(lane < tail, gl, 0.0)
        GL[h, ch] = gl.astype(BF16)
        g_copy(ch).start()

    def c_copy(g):
        return copy(GT.at[g, :, :, 1 - c], RC.at[g], cs.at[g], cr.at[g], sibling)

    def x_copy(g, k):
        to = lax.rem(x + k, 4)
        return copy(X1.at[g, to], RX.at[g, k - 1], xs.at[g * 3 + k - 1], xr.at[g * 3 + k - 1],
                    at_e(to * 2 + c))

    def rz_copy(g, i):
        return copy(X2.at[g, i], RZ.at[zl], rzs.at[g * 4 + i], rzr.at[zl], at_z(g * 8 + h * 4 + i))

    for g in (h, oh):
        if g is oh:
            for ch in range(NC):
                sl = GL.at[oh, ch]
                copy(sl, sl, gs.at[ch], gr.at[ch], partner).wait_recv()

        def mm(i, _):
            for half in range(2):
                r0 = pl.multiple_of(i * KS + half * 320, 320)
                tot = jnp.zeros((320, TK), F32)
                for ch in range(NC):
                    tot = tot + lax.dot_general(
                        Wc[ch, pl.ds(r0, 320), :], GL[g, ch], (((1,), (1,)), ((), ())),
                        preferred_element_type=F32)
                GT[g, i, 2 * half:2 * half + 2] = tot.reshape(2, 2, OB, TK)
            return _

        lax.fori_loop(0, 4, mm, 0)
        c_copy(g).start()
        c_copy(g).wait_recv()

        def add_c(i, _):
            for xx in range(4):
                X1[g, xx, i] = GT[g, i, xx, c] + RC[g, i, xx]
            return _

        lax.fori_loop(0, 4, add_c, 0)
        for k in (1, 3, 2):
            x_copy(g, k).start()
        for k in (1, 2, 3):
            x_copy(g, k).wait_recv()

        def add_x(i, _):
            X2[g, i] = X1[g, x, i] + RX[g, 0, i] + RX[g, 1, i] + RX[g, 2, i]
            return _

        lax.fori_loop(0, 4, add_x, 0)

        def rz_send(i, _):
            dst = g * 8 + h * 4 + i

            @pl.when(dst != z)
            def _go():
                rz_copy(g, i).start()

            @pl.when(dst == z)
            def _own():
                RZ[zl] = X2[g, i]
            return _

        lax.fori_loop(0, 4, rz_send, 0)

    def rz_wait(k, _):
        @pl.when(hb * 8 + k != z)
        def _go():
            copy(X2.at[0, 0], RZ.at[k], rzs.at[0], rzr.at[k], partner).wait_recv()
        return _

    lax.fori_loop(0, 8, rz_wait, 0)
    tot = RZ[0]
    for k in range(1, 8):
        tot = tot + RZ[k]
    out_ref[...] = tot

    def s1_done(k, _):
        @pl.when(hb * 8 + k != z)
        def _go():
            feat_copy(k).wait_send()
        return _

    lax.fori_loop(0, 8, s1_done, 0)

    def w_done(ch, _):
        for k in (1, 2, 3):
            w_copy(ch, k).wait_send()
        z_copy(ch).wait_send()
        g_copy(ch).wait_send()
        return _

    lax.fori_loop(0, NC, w_done, 0)

    def p_done(k, _):
        ta_copy(k).wait_send()
        tb_copy(k).wait_send()
        sa_copy(k).wait_send()
        sb_copy(k).wait_send()
        return _

    lax.fori_loop(1, 8, p_done, 0)

    def g_done(g, _):
        for k in (1, 2, 3):
            s2_copy(g, k).wait_send()
            x_copy(g, k).wait_send()
        s3_copy(g).wait_send()
        c_copy(g).wait_send()
        for i in range(4):
            @pl.when(g * 8 + h * 4 + i != z)
            def _go():
                rz_copy(g, i).wait_send()
        return _

    lax.fori_loop(0, 2, g_done, 0)


def on_device(hidden, head_weight, teacher_logits, block_owner, sampled_ids, loss_weight):
    number = jnp.arange(64, dtype=jnp.int32)
    inv = jnp.sum(jnp.where(block_owner[None, :] == number[:, None], number[None, :], 0), axis=1).astype(jnp.int32)
    hid = hidden.reshape(8, 8, 2, OB).transpose(3, 1, 0, 2).reshape(OB, TK)
    ids = sampled_ids.reshape(8, 8, 2).transpose(1, 0, 2).reshape(TK, 1)
    lw = loss_weight.reshape(8, 8, 2).transpose(1, 0, 2).reshape(TK, 1)
    tea = teacher_logits.reshape(2, 64, VD).transpose(1, 0, 2).astype(F32)
    tea = jnp.pad(tea, ((0, 0), (0, 0), (0, VP - VD)))
    vm = pl.BlockSpec(memory_space=pltpu.VMEM)
    dma = pltpu.SemaphoreType.DMA
    out, tok = pl.pallas_call(
        kernel,
        out_shape=[jax.ShapeDtypeStruct((OB, TK), F32), jax.ShapeDtypeStruct((8, TK), F32)],
        in_specs=[pl.BlockSpec(memory_space=pltpu.SMEM)] + [vm] * 5,
        out_specs=[vm, vm],
        scratch_shapes=[
            pltpu.VMEM((2, 4, 4, 2, OB, TK), BF16),
            pltpu.VMEM((2, TK, KH), BF16),
            pltpu.VMEM((NC, KH, VC), BF16),
            pltpu.VMEM((NC, TK, VC), F32),
            pltpu.VMEM((NC, TK, VC), F32),
            pltpu.VMEM((NC, TK, VC), F32),
            pltpu.VMEM((16, VP), F32),
            pltpu.VMEM((8, 16, VP), BF16),
            pltpu.VMEM((8, 16, VP), BF16),
            pltpu.VMEM((8, 16, VP), F32),
            pltpu.VMEM((8, 16, VP), BF16),
            pltpu.VMEM((8, 16, VP), BF16),
            pltpu.VMEM((8, TK), F32),
            pltpu.VMEM((8, 8, TK), F32),
            pltpu.VMEM((8, TK), F32),
            pltpu.VMEM((8, 8, TK), F32),
            pltpu.VMEM((128, TK), F32),
            pltpu.VMEM((2, NC, TK, VC), BF16),
            pltpu.VMEM((2, 4, 4, 2, OB, TK), F32),
            pltpu.VMEM((2, 4, 4, OB, TK), F32),
            pltpu.VMEM((2, 4, 4, OB, TK), F32),
            pltpu.VMEM((2, 3, 4, OB, TK), F32),
            pltpu.VMEM((2, 4, OB, TK), F32),
            pltpu.VMEM((8, OB, TK), F32),
            dma((8,)), dma((8,)),
            dma((6,)), dma((6,)),
            dma((2,)), dma((2,)),
            dma((3 * NC,)), dma((3 * NC,)),
            dma((NC,)), dma((NC,)),
            dma((7,)), dma((7,)),
            dma((7,)), dma((7,)),
            dma((7,)), dma((7,)),
            dma((7,)), dma((7,)),
            dma((NC,)), dma((NC,)),
            dma((2,)), dma((2,)),
            dma((6,)), dma((6,)),
            dma((8,)), dma((8,)),
        ],
        compiler_params=pltpu.CompilerParams(
            collective_id=0, has_side_effects=True, vmem_limit_bytes=56 * 2**20
        ),
    )(inv, hid, head_weight, tea, ids, lw)
    grad = out.reshape(OB, 8, 8, 2).transpose(2, 1, 3, 0).reshape(TK, OB)
    tok = tok[0:2].reshape(2, 8, 8, 2).transpose(0, 2, 1, 3).reshape(2, TK)
    return grad, tok[0], tok[1]


def solution(mesh):
    return jax.shard_map(
        on_device,
        mesh=mesh,
        in_specs=(
            P("dp", "vocab"),
            P("dp", "vocab"),
            P(("dp", "vocab"), None),
            P(),
            P("dp"),
            P("dp"),
        ),
        out_specs=(P("dp", "vocab"), P("dp"), P("dp")),
        check_vma=False,
    )
```

```python
import jax
import jax.numpy as jnp
from jax import lax
from jax.experimental import pallas as pl
from jax.experimental.pallas import tpu as pltpu
from jax.sharding import PartitionSpec as P

MESH = pl.DeviceIdType.MESH
F32 = jnp.float32
BF16 = jnp.bfloat16

VD = 1188
VC = 240
NC = 5
VQ = VC * NC
VP = 1280
TAIL = VD - (NC - 1) * VC
KS = 640
KH = 4 * KS
TK = 128
OB = 80
WIN = VP + 128


def kernel(
    own_ref, hT, w_ref, tea_ref, ids_ref, lw_ref,
    out_ref,
    Wv, Ow, TJ, Hb, Wc, Sb, Rb, L, TP, TQ, TR, TT, TN,
    St, StA, St2, StB, GA, GL, GT, RC, X1, RX, X2, RQ, Qs, RZ,
    lds, s1s, s1r, s2s, s2r, s3s, s3r, ws, wr, fs, fr, zs_, zr_,
    tas, tar, tbs, tbr, sas, sar, sbs, sbr, gs, gr, cs, cr, xs, xr, rqs, rqr, rzs, rzr,
):
    dp = lax.axis_index("dp")
    v = lax.axis_index("vocab")
    h = lax.div(dp, 4)
    q = lax.rem(dp, 4)
    zl = lax.div(v, 8)
    e = lax.rem(v, 8)
    x = lax.div(e, 2)
    c = lax.rem(e, 2)
    z = h * 8 + zl
    oh = 1 - h
    hb = lax.div(zl, 4)
    ip = lax.rem(zl, 4)
    done = []

    def at_z(zz):
        return (lax.div(zz, 8) * 4 + q, lax.rem(zz, 8) * 8 + e)

    def at_y(yy):
        return (h * 4 + yy, v)

    def at_e(ee):
        return (dp, zl * 8 + ee)

    partner = at_z(oh * 8 + zl)
    sibling = at_e(x * 2 + 1 - c)

    def copy(src, dst, ss, rs, dev):
        return pltpu.make_async_remote_copy(
            src_ref=src, dst_ref=dst, send_sem=ss, recv_sem=rs, device_id=dev, device_id_type=MESH
        )

    def loop(lo, hi, body):
        def step(k, carry):
            body(k)
            return carry
        lax.fori_loop(lo, hi, step, 0)

    load_w = pltpu.make_async_copy(w_ref, Wv, lds)
    load_w.start()
    barrier = pltpu.get_barrier_semaphore()

    def greet(dev):
        pl.semaphore_signal(barrier, inc=1, device_id=dev, device_id_type=MESH)

    loop(1, 16, lambda k: greet(at_z(lax.rem(z + k, 16))))
    loop(1, 4, lambda k: greet(at_y(lax.rem(q + k, 4))))
    loop(1, 8, lambda k: greet(at_e(lax.rem(e + k, 8))))

    load_w.wait()
    full = VD // 16 * 16
    Wc[q, 0:full] = Wv[0:full]
    last = Wv[full:VD].astype(F32)
    Wc[q, full:VQ] = jnp.concatenate([last, jnp.zeros((VQ - VD, KS), F32)], axis=0).astype(BF16)

    def unpack(j):
        s = j * VD
        a = pl.multiple_of(jnp.minimum(lax.div(s, 128) * 128, 64 * VD - WIN), 128)
        win = tea_ref[:, pl.ds(a, WIN)].astype(F32)
        win = pltpu.roll(win, WIN - (s - a), 1)
        TJ[pl.ds(j, 1), :] = win[0:1, 0:VP]
        TJ[pl.ds(64 + j, 1), :] = win[1:2, 0:VP]

    loop(0, 64, unpack)
    Ow[:, 0:64] = own_ref[...]
    Ow[:, 64:128] = own_ref[...]
    r_i = lax.broadcasted_iota(jnp.int32, (128, 128), 0)
    c_i = lax.broadcasted_iota(jnp.int32, (128, 128), 1)

    def permute(mask, rows):
        return jnp.dot(mask.astype(F32).astype(BF16), rows, preferred_element_type=F32).astype(BF16)

    block = (r_i // 16) * 8 + r_i % 8
    pick = jnp.logical_and((r_i // 8) % 2 == c_i // 64, Ow[...] == block)
    TP[...] = permute(pick, TJ[...].astype(BF16)).reshape(8, 16, VP)

    pl.semaphore_wait(barrier, 25)

    def feat_copy(k):
        return copy(hT, Hb.at[h, ip, x, c], s1s.at[k], s1r.at[h * 4 + ip], at_z(hb * 8 + k))

    def not_self(k, fn):
        @pl.when(hb * 8 + k != z)
        def _go():
            fn(k)

    loop(0, 8, lambda k: not_self(k, lambda k: feat_copy(k).start()))
    done.append(lambda: loop(0, 8, lambda k: not_self(k, lambda k: feat_copy(k).wait_send())))

    @pl.when(hb == h)
    def _own():
        Hb[h, ip, x, c] = hT[...]

    def w_part(ch, yy, lo, n):
        rows = pl.ds(pl.multiple_of(ch * VC + lo, 16), n)
        return Wc.at[lax.rem(yy, 4), rows]

    HALF = (0, 128), (128, VC - 128)

    def w_copy(ch, k):
        sl = w_part(ch, q, 0, VC)
        n = ch * 2 + k // 2
        return copy(sl, sl, ws.at[n], wr.at[n], at_y(lax.rem(q + k, 4)))

    def w_from(ch, k):
        sl = w_part(ch, q + 4 - k, 0, VC)
        n = ch * 2 + k // 2
        return copy(sl, sl, ws.at[n], wr.at[n], partner)

    def f_copy(ch, k):
        sl = w_part(ch, q + 4 - k, *HALF[k // 2])
        n = ch * 2 + k // 2
        return copy(sl, sl, fs.at[n], fr.at[n], at_y(lax.rem(q + k, 4)))

    def f_from(ch, k):
        sl = w_part(ch, q + 2, *HALF[k // 2])
        n = ch * 2 + k // 2
        return copy(sl, sl, fs.at[n], fr.at[n], partner)

    def w_send(ch):
        for k in (1, 3):
            w_copy(ch, k).start()

    def w_pass(ch):
        for k in (1, 3):
            w_from(ch, k).wait_recv()
            f_copy(ch, k).start()

        @pl.when(ch + 1 < NC)
        def _more():
            w_send(ch + 1)

    def w_done(ch):
        for k in (1, 3):
            w_copy(ch, k).wait_send()
            f_copy(ch, k).wait_send()

    w_send(0)
    done.append(lambda: loop(0, NC, w_done))

    def s2_copy(g, k):
        sl = Hb.at[g, :, x, c]
        return copy(sl, sl, s2s.at[g * 3 + k - 1], s2r.at[g * 3 + k - 1],
                    at_e(lax.rem(x + k, 4) * 2 + c))

    def s2_from(g, k):
        sl = Hb.at[g, :, lax.rem(x + 4 - k, 4), c]
        return copy(sl, sl, s2s.at[g * 3 + k - 1], s2r.at[g * 3 + k - 1], partner)

    def s3_copy(g):
        sl = Hb.at[g, :, :, c]
        return copy(sl, sl, s3s.at[g], s3r.at[g], sibling)

    def s3_from(g):
        sl = Hb.at[g, :, :, 1 - c]
        return copy(sl, sl, s3s.at[g], s3r.at[g], sibling)

    for g in (oh, h):
        def s1_wait(i):
            @pl.when(g * 8 + h * 4 + i != z)
            def _go():
                copy(hT, Hb.at[g, i, x, c], s1s.at[0], s1r.at[g * 4 + i], partner).wait_recv()

        loop(0, 4, s1_wait)
        for k in (1, 3, 2):
            s2_copy(g, k).start()

    def ta_copy(k):
        to = lax.rem(zl + k, 8)
        return copy(TP.at[to], TQ.at[zl], tas.at[k - 1], tar.at[k - 1], at_z(h * 8 + to))

    loop(1, 8, lambda k: ta_copy(k).start())
    done.append(lambda: loop(1, 8, lambda k: ta_copy(k).wait_send()))
    TQ[zl] = TP[zl]

    w_pass(0)
    for g in (oh, h):
        for k in (1, 3, 2):
            s2_from(g, k).wait_recv()
        s3_copy(g).start()
    w_pass(1)
    s3_from(oh).wait_recv()

    def s_done(g):
        for k in (1, 2, 3):
            s2_copy(g, k).wait_send()
        s3_copy(g).wait_send()

    done.append(lambda: loop(0, 2, s_done))

    def z_copy(ch):
        return copy(Sb.at[ch], Rb.at[ch], zs_.at[ch], zr_.at[ch], partner)

    def rows_of(ch):
        return pl.ds(pl.multiple_of(ch * VC, 16), VC)

    def part(g, ch):
        tot = None
        for i in range(4):
            one = jnp.dot(Wc[i, rows_of(ch)], Hb[g, i].reshape(KS, TK), preferred_element_type=F32)
            tot = one if tot is None else tot + one
        return tot

    def chunk(ch):
        for k in (1, 3):
            f_from(ch, k).wait_recv()
        Sb[ch] = part(oh, ch)
        z_copy(ch).start()

        @pl.when(ch + 2 < NC)
        def _next():
            w_pass(ch + 2)

        @pl.when(ch == 0)
        def _feat():
            s3_from(h).wait_recv()

        L[ch] = part(h, ch)

    loop(0, NC, chunk)
    done.append(lambda: loop(0, NC, lambda ch: z_copy(ch).wait_send()))

    def ta_wait(k):
        frm = lax.rem(zl + 8 - k, 8)
        copy(TP.at[0], TQ.at[frm], tas.at[k - 1], tar.at[k - 1], partner).wait_recv()

    loop(1, 8, ta_wait)
    pick = jnp.logical_and(
        r_i // 16 == c_i % 8,
        jnp.logical_and((r_i // 2) % 8 == c_i // 16, r_i % 2 == (c_i // 8) % 2))
    TR[...] = permute(pick, TQ[...].reshape(TK, VP)).reshape(8, 16, VP)

    def tb_copy(k):
        to = lax.rem(e + k, 8)
        return copy(TR.at[to], TT.at[e], tbs.at[k - 1], tbr.at[k - 1], at_e(to))

    def tb_wait(k):
        frm = lax.rem(e + 8 - k, 8)
        copy(TR.at[0], TT.at[frm], tbs.at[k - 1], tbr.at[k - 1], sibling).wait_recv()

    loop(1, 8, lambda k: tb_copy(k).start())
    done.append(lambda: loop(1, 8, lambda k: tb_copy(k).wait_send()))
    TT[e] = TR[e]
    here = ids_ref[...] - v * VD
    lw = lw_ref[...]
    loop(1, 8, tb_wait)
    pick = jnp.logical_and(
        c_i // 16 == (r_i // 2) % 8,
        jnp.logical_and((c_i // 2) % 8 == r_i // 16, c_i % 2 == r_i % 2))
    TN[...] = lax.dot_general(
        TT[...].reshape(TK, VP), pick.astype(F32).astype(BF16), (((0,), (0,)), ((), ())),
        preferred_element_type=F32)

    lane = lax.broadcasted_iota(jnp.int32, (VC, TK), 0)
    low = F32(-3.0e38)

    def tea(ch):
        return TN[ch * VC:(ch + 1) * VC, :]

    m_s = jnp.full((1, TK), low, F32)
    m_t = jnp.full((1, TK), low, F32)
    for ch in range(NC):
        z_copy(ch).wait_recv()
        val = L[ch] + Rb[ch]
        L[ch] = val
        t = tea(ch)
        if ch == NC - 1:
            val = jnp.where(lane < TAIL, val, low)
            t = jnp.where(lane < TAIL, t, low)
        m_s = jnp.maximum(m_s, jnp.max(val, axis=0, keepdims=True))
        m_t = jnp.maximum(m_t, jnp.max(t, axis=0, keepdims=True))

    s_sum = jnp.zeros((1, TK), F32)
    s_gap = jnp.zeros((1, TK), F32)
    s_pick = jnp.zeros((1, TK), F32)
    s_tea = jnp.zeros((1, TK), F32)
    for ch in range(NC):
        val = L[ch]
        t = tea(ch)
        ex = jnp.exp(val - m_s)
        et = jnp.exp(t - m_t)
        eg = ex * (val - t)
        pk = jnp.where(lane + ch * VC == here, val, 0.0)
        if ch == NC - 1:
            ok = lane < TAIL
            ex = jnp.where(ok, ex, 0.0)
            et = jnp.where(ok, et, 0.0)
            eg = jnp.where(ok, eg, 0.0)
            pk = jnp.where(ok, pk, 0.0)
        s_sum = s_sum + jnp.sum(ex, axis=0, keepdims=True)
        s_gap = s_gap + jnp.sum(eg, axis=0, keepdims=True)
        s_pick = s_pick + jnp.sum(pk, axis=0, keepdims=True)
        s_tea = s_tea + jnp.sum(et, axis=0, keepdims=True)

    row = lax.broadcasted_iota(jnp.int32, (8, TK), 0)

    def stack(vals):
        acc = jnp.zeros((8, TK), F32)
        for n, val in enumerate(vals):
            acc = jnp.where(row == n, val, acc)
        return acc

    St[...] = stack((m_s, s_sum, s_gap, s_pick, m_t, s_tea))

    def combine(ref):
        ms = ref[0, 0:1]
        mt = ref[0, 4:5]
        for j in range(1, 8):
            ms = jnp.maximum(ms, ref[j, 0:1])
            mt = jnp.maximum(mt, ref[j, 4:5])
        a = b = p = t = jnp.zeros((1, TK), F32)
        for j in range(8):
            f = jnp.exp(ref[j, 0:1] - ms)
            a = a + ref[j, 1:2] * f
            b = b + ref[j, 2:3] * f
            p = p + ref[j, 3:4]
            t = t + ref[j, 5:6] * jnp.exp(ref[j, 4:5] - mt)
        return ms, a, b, p, mt, t

    def sa_copy(k):
        return copy(St, StA.at[e], sas.at[k - 1], sar.at[k - 1], at_e(lax.rem(e + k, 8)))

    def sa_wait(k):
        copy(St, StA.at[lax.rem(e + 8 - k, 8)], sas.at[k - 1], sar.at[k - 1], sibling).wait_recv()

    loop(1, 8, lambda k: sa_copy(k).start())
    done.append(lambda: loop(1, 8, lambda k: sa_copy(k).wait_send()))
    StA[e] = St[...]
    loop(1, 8, sa_wait)
    St2[...] = stack(combine(StA))

    def sb_copy(k):
        return copy(St2, StB.at[zl], sbs.at[k - 1], sbr.at[k - 1], at_z(h * 8 + lax.rem(zl + k, 8)))

    def sb_wait(k):
        copy(St2, StB.at[lax.rem(zl + 8 - k, 8)], sbs.at[k - 1], sbr.at[k - 1], sibling).wait_recv()

    loop(1, 8, lambda k: sb_copy(k).start())
    done.append(lambda: loop(1, 8, lambda k: sb_copy(k).wait_send()))
    StB[zl] = St2[...]
    loop(1, 8, sb_wait)
    ms, a, b, p, mt, t = combine(StB)
    s_lse = ms + jnp.log(a)
    t_lse = mt + jnp.log(t)
    div = b / a - s_lse + t_lse
    out_ref[OB:OB + 8, :] = stack((div, p - s_lse))

    def g_copy(ch):
        sl = GL.at[h, ch]
        return copy(sl, sl, gs.at[ch], gr.at[ch], partner)

    def g_wait(ch):
        sl = GL.at[oh, ch]
        copy(sl, sl, gs.at[ch], gr.at[ch], partner).wait_recv()

    for ch in range(NC):
        val = L[ch]
        gl = lw * jnp.exp(val - s_lse) * ((val - tea(ch)) - s_lse + t_lse - div)
        if ch == NC - 1:
            gl = jnp.where(lane < TAIL, gl, 0.0)
        GL[h, ch] = gl.astype(BF16)
        g_copy(ch).start()
    done.append(lambda: loop(0, NC, lambda ch: g_copy(ch).wait_send()))
    def c_copy(g, i):
        n = g * 4 + i
        return copy(GT.at[g, i, :, 1 - c], RC.at[g, i], cs.at[n], cr.at[n], sibling)

    def x_copy(g, i, k):
        to = lax.rem(x + k, 4)
        n = (g * 4 + i) * 3 + k - 1
        return copy(X1.at[g, i, to], RX.at[g, i, k - 1], xs.at[n], xr.at[n], at_e(to * 2 + c))

    def rq_copy(g, i):
        return copy(X2.at[g, i], RQ.at[g, ip], rqs.at[g * 4 + i], rqr.at[g * 4 + ip],
                    at_z(h * 8 + hb * 4 + i))

    def rz_copy(g):
        return copy(Qs.at[g], RZ.at[hb], rzs.at[g], rzr.at[hb], at_z(g * 8 + h * 4 + ip))

    def x_stage(g, i):
        c_copy(g, i).wait_recv()
        for xx in range(4):
            X1[g, i, xx] = GT[g, i, xx, c] + RC[g, i, xx]
        for k in (2, 1, 3):
            x_copy(g, i, k).start()

    def x_sum(g, i):
        for k in (1, 3, 2):
            x_copy(g, i, k).wait_recv()
        X2[g, i] = X1[g, i, x] + RX[g, i, 0] + RX[g, i, 1] + RX[g, i, 2]

    def not_me(i, fn):
        @pl.when(i != ip)
        def _go():
            fn()

    def q_stage(g, i):
        not_me(i, lambda: rq_copy(g, i).start())

        @pl.when(i == ip)
        def _own():
            RQ[g, ip] = X2[g, i]

    def z_stage(g):
        def q_wait(i):
            not_me(i, lambda: copy(
                X2.at[g, 0], RQ.at[g, i], rqs.at[0], rqr.at[g * 4 + i], partner).wait_recv())

        loop(0, 4, q_wait)
        Qs[g] = RQ[g, 0] + RQ[g, 1] + RQ[g, 2] + RQ[g, 3]
        dst = g * 8 + h * 4 + ip

        @pl.when(dst != z)
        def _go():
            rz_copy(g).start()

        @pl.when(dst == z)
        def _own():
            RZ[hb] = Qs[g]

    def mm(g, i, chs):
        tot = None
        for ch in chs:
            one = lax.dot_general(
                GL[g, ch], Wc[i, ch * VC:(ch + 1) * VC],
                (((0,), (0,)), ((), ())), preferred_element_type=F32)
            tot = one if tot is None else tot + one
        return tot

    def to_send(g, i, tot):
        GT[g, i] = tot.T.reshape(4, 2, OB, TK)
        c_copy(g, i).start()

    def own_mm(i):
        to_send(h, i, mm(h, i, range(NC)))

    loop(0, 4, own_mm)
    loop(0, 4, lambda i: x_stage(h, i))
    loop(0, 4, lambda i: x_sum(h, i))

    g_wait(0)
    g_wait(1)

    def oth_a(i):
        GA[i] = mm(oh, i, (0, 1))

    def oth_b(i):
        GA[i] = GA[i] + mm(oh, i, (2, 3))

    def oth_c(i):
        to_send(oh, i, GA[i] + mm(oh, i, (4,)))

    loop(0, 4, oth_a)
    g_wait(2)
    g_wait(3)
    loop(0, 4, oth_b)
    g_wait(4)
    loop(0, 4, lambda i: q_stage(h, i))
    loop(0, 4, oth_c)
    loop(0, 4, lambda i: x_stage(oh, i))
    z_stage(h)

    def tail(i):
        x_sum(oh, i)
        q_stage(oh, i)

    loop(0, 4, tail)
    z_stage(oh)

    def rz_wait(r):
        @pl.when(hb * 8 + r * 4 + ip != z)
        def _go():
            copy(Qs.at[0], RZ.at[r], rzs.at[0], rzr.at[r], partner).wait_recv()

    loop(0, 2, rz_wait)
    out_ref[0:OB, :] = RZ[0] + RZ[1]

    def rs_done(n):
        g = lax.div(n, 4)
        i = lax.rem(n, 4)
        c_copy(g, i).wait_send()
        for k in (1, 2, 3):
            x_copy(g, i, k).wait_send()

        not_me(i, lambda: rq_copy(g, i).wait_send())

    def rz_done(g):
        @pl.when(g * 8 + h * 4 + ip != z)
        def _go():
            rz_copy(g).wait_send()

    done.append(lambda: loop(0, 8, rs_done))
    done.append(lambda: loop(0, 2, rz_done))

    for fn in done:
        fn()


def split(both_ref, grad_ref, div_ref, slp_ref):
    grad_ref[...] = both_ref[0:OB, :]
    div_ref[...] = both_ref[OB:OB + 1, :]
    slp_ref[...] = both_ref[OB + 1:OB + 2, :]


def on_device(hidden, head_weight, teacher_logits, block_owner, sampled_ids, loss_weight):
    vm = pl.BlockSpec(memory_space=pltpu.VMEM)
    dma = pltpu.SemaphoreType.DMA
    both = pl.pallas_call(
        kernel,
        out_shape=jax.ShapeDtypeStruct((OB + 8, TK), F32),
        in_specs=[vm, vm, pl.BlockSpec(memory_space=pl.ANY), vm, vm, vm],
        out_specs=vm,
        scratch_shapes=[
            pltpu.VMEM((VD, KS), BF16),
            pltpu.VMEM((1, 128), jnp.int32),
            pltpu.VMEM((128, VP), F32),
            pltpu.VMEM((2, 4, 4, 2, OB, TK), BF16),
            pltpu.VMEM((4, VQ, KS), BF16),
            pltpu.VMEM((NC, VC, TK), F32),
            pltpu.VMEM((NC, VC, TK), F32),
            pltpu.VMEM((NC, VC, TK), F32),
            pltpu.VMEM((8, 16, VP), BF16),
            pltpu.VMEM((8, 16, VP), BF16),
            pltpu.VMEM((8, 16, VP), BF16),
            pltpu.VMEM((8, 16, VP), BF16),
            pltpu.VMEM((VP, TK), F32),
            pltpu.VMEM((8, TK), F32),
            pltpu.VMEM((8, 8, TK), F32),
            pltpu.VMEM((8, TK), F32),
            pltpu.VMEM((8, 8, TK), F32),
            pltpu.VMEM((4, TK, KS), F32),
            pltpu.VMEM((2, NC, VC, TK), BF16),
            pltpu.VMEM((2, 4, 4, 2, OB, TK), F32),
            pltpu.VMEM((2, 4, 4, OB, TK), F32),
            pltpu.VMEM((2, 4, 4, OB, TK), F32),
            pltpu.VMEM((2, 4, 3, OB, TK), F32),
            pltpu.VMEM((2, 4, OB, TK), F32),
            pltpu.VMEM((2, 4, OB, TK), F32),
            pltpu.VMEM((2, OB, TK), F32),
            pltpu.VMEM((2, OB, TK), F32),
            dma,
            dma((8,)), dma((8,)),
            dma((6,)), dma((6,)),
            dma((2,)), dma((2,)),
            dma((2 * NC,)), dma((2 * NC,)),
            dma((2 * NC,)), dma((2 * NC,)),
            dma((NC,)), dma((NC,)),
            dma((7,)), dma((7,)),
            dma((7,)), dma((7,)),
            dma((7,)), dma((7,)),
            dma((7,)), dma((7,)),
            dma((NC,)), dma((NC,)),
            dma((8,)), dma((8,)),
            dma((24,)), dma((24,)),
            dma((8,)), dma((8,)),
            dma((2,)), dma((2,)),
        ],
        compiler_params=pltpu.CompilerParams(
            collective_id=0, has_side_effects=True, vmem_limit_bytes=56 * 2**20
        ),
    )(block_owner.reshape(1, 64), hidden.T, head_weight.T, teacher_logits,
      sampled_ids.reshape(1, TK), loss_weight.reshape(1, TK))
    grad, div, slp = pl.pallas_call(
        split,
        out_shape=[
            jax.ShapeDtypeStruct((OB, TK), F32),
            jax.ShapeDtypeStruct((1, TK), F32),
            jax.ShapeDtypeStruct((1, TK), F32),
        ],
        in_specs=[vm],
        out_specs=[vm, vm, vm],
    )(both)
    return grad.T, div.reshape(TK), slp.reshape(TK)


def solution(mesh):
    return jax.shard_map(
        on_device,
        mesh=mesh,
        in_specs=(
            P("dp", "vocab"),
            P("dp", "vocab"),
            P(("dp", "vocab"), None),
            P(),
            P("dp"),
            P("dp"),
        ),
        out_specs=(P("dp", "vocab"), P("dp"), P("dp")),
        check_vma=False,
    )
```

```python
import jax
import jax.numpy as jnp
from jax import lax
from jax.experimental import pallas as pl
from jax.experimental.pallas import tpu as pltpu
from jax.sharding import PartitionSpec as P

MESH = pl.DeviceIdType.MESH
F32 = jnp.float32
BF16 = jnp.bfloat16

VD = 1188
VC = 240
NC = 5
VQ = VC * NC
VP = 1280
TAIL = VD - (NC - 1) * VC
KS = 640
KH = 4 * KS
TK = 128
OB = 80
WIN = VP + 128


def kernel(
    own_ref, hT, w_ref, tea_ref, ids_ref, lw_ref,
    out_ref,
    Wv, Tv, Ow, TJ, Hb, Wc, Sb, Rb, L, TP, TQ, TR, TT, TN,
    St, StA, St2, StB, GA, GL, GT, RC, X1, RX, X2, RQ, Qs, RZ,
    lds, ldt, s1s, s1r, s2s, s2r, s3s, s3r, ws, wr, fs, fr, zs_, zr_,
    tas, tar, tbs, tbr, sas, sar, sbs, sbr, gs, gr, cs, cr, xs, xr, rqs, rqr, rzs, rzr,
):
    dp = lax.axis_index("dp")
    v = lax.axis_index("vocab")
    h = lax.div(dp, 4)
    q = lax.rem(dp, 4)
    zl = lax.div(v, 8)
    e = lax.rem(v, 8)
    x = lax.div(e, 2)
    c = lax.rem(e, 2)
    z = h * 8 + zl
    oh = 1 - h
    hb = lax.div(zl, 4)
    ip = lax.rem(zl, 4)
    done = []

    def at_z(zz):
        return (lax.div(zz, 8) * 4 + q, lax.rem(zz, 8) * 8 + e)

    def at_y(yy):
        return (h * 4 + yy, v)

    def at_e(ee):
        return (dp, zl * 8 + ee)

    partner = at_z(oh * 8 + zl)
    sibling = at_e(x * 2 + 1 - c)

    def copy(src, dst, ss, rs, dev):
        return pltpu.make_async_remote_copy(
            src_ref=src, dst_ref=dst, send_sem=ss, recv_sem=rs, device_id=dev, device_id_type=MESH
        )

    def loop(lo, hi, body):
        def step(k, carry):
            body(k)
            return carry
        lax.fori_loop(lo, hi, step, 0)

    load_w = pltpu.make_async_copy(w_ref, Wv, lds)
    load_w.start()
    load_t = pltpu.make_async_copy(tea_ref, Tv, ldt)
    load_t.start()
    barrier = pltpu.get_barrier_semaphore()

    def greet(dev):
        pl.semaphore_signal(barrier, inc=1, device_id=dev, device_id_type=MESH)

    loop(1, 16, lambda k: greet(at_z(lax.rem(z + k, 16))))
    loop(1, 4, lambda k: greet(at_y(lax.rem(q + k, 4))))
    loop(1, 8, lambda k: greet(at_e(lax.rem(e + k, 8))))

    pl.semaphore_wait(barrier, 25)

    def feat_copy(k):
        return copy(hT, Hb.at[h, ip, x, c], s1s.at[k], s1r.at[h * 4 + ip], at_z(hb * 8 + k))

    def not_self(k, fn):
        @pl.when(hb * 8 + k != z)
        def _go():
            fn(k)

    loop(0, 8, lambda k: not_self(k, lambda k: feat_copy(k).start()))
    done.append(lambda: loop(0, 8, lambda k: not_self(k, lambda k: feat_copy(k).wait_send())))

    @pl.when(hb == h)
    def _own():
        Hb[h, ip, x, c] = hT[...]

    load_w.wait()
    full = VD // 16 * 16
    Wc[q, 0:full] = Wv[0:full]
    last = Wv[full:VD].astype(F32)
    Wc[q, full:VQ] = jnp.concatenate([last, jnp.zeros((VQ - VD, KS), F32)], axis=0).astype(BF16)


    def w_part(ch, yy, lo, n):
        rows = pl.ds(pl.multiple_of(ch * VC + lo, 16), n)
        return Wc.at[lax.rem(yy, 4), rows]

    HALF = (0, 128), (128, VC - 128)

    def w_copy(ch, k):
        sl = w_part(ch, q, 0, VC)
        n = ch * 2 + k // 2
        return copy(sl, sl, ws.at[n], wr.at[n], at_y(lax.rem(q + k, 4)))

    def w_from(ch, k):
        sl = w_part(ch, q + 4 - k, 0, VC)
        n = ch * 2 + k // 2
        return copy(sl, sl, ws.at[n], wr.at[n], partner)

    def f_copy(ch, k):
        sl = w_part(ch, q + 4 - k, *HALF[k // 2])
        n = ch * 2 + k // 2
        return copy(sl, sl, fs.at[n], fr.at[n], at_y(lax.rem(q + k, 4)))

    def f_from(ch, k):
        sl = w_part(ch, q + 2, *HALF[k // 2])
        n = ch * 2 + k // 2
        return copy(sl, sl, fs.at[n], fr.at[n], partner)

    def w_send(ch):
        for k in (1, 3):
            w_copy(ch, k).start()

    def w_pass(ch):
        for k in (1, 3):
            w_from(ch, k).wait_recv()
            f_copy(ch, k).start()

        @pl.when(ch + 2 < NC)
        def _more():
            w_send(ch + 2)

    def w_done(ch):
        for k in (1, 3):
            w_copy(ch, k).wait_send()
            f_copy(ch, k).wait_send()

    w_send(0)
    w_send(1)
    done.append(lambda: loop(0, NC, w_done))

    load_t.wait()

    def unpack(j):
        s = j * VD
        a = pl.multiple_of(jnp.minimum(lax.div(s, 128) * 128, 64 * VD - WIN), 128)
        win = Tv[:, pl.ds(a, WIN)].astype(F32)
        win = pltpu.roll(win, WIN - (s - a), 1)
        TJ[pl.ds(j, 1), :] = win[0:1, 0:VP]
        TJ[pl.ds(64 + j, 1), :] = win[1:2, 0:VP]

    loop(0, 64, unpack)
    Ow[:, 0:64] = own_ref[...]
    Ow[:, 64:128] = own_ref[...]
    r_i = lax.broadcasted_iota(jnp.int32, (128, 128), 0)
    c_i = lax.broadcasted_iota(jnp.int32, (128, 128), 1)

    def permute(mask, rows):
        return jnp.dot(mask.astype(F32).astype(BF16), rows, preferred_element_type=F32).astype(BF16)

    block = (r_i // 16) * 8 + r_i % 8
    pick = jnp.logical_and((r_i // 8) % 2 == c_i // 64, Ow[...] == block)
    TP[...] = permute(pick, TJ[...].astype(BF16)).reshape(8, 16, VP)

    def ta_copy(k):
        to = lax.rem(zl + k, 8)
        return copy(TP.at[to], TQ.at[zl], tas.at[k - 1], tar.at[k - 1], at_z(h * 8 + to))

    loop(1, 8, lambda k: ta_copy(k).start())
    done.append(lambda: loop(1, 8, lambda k: ta_copy(k).wait_send()))
    TQ[zl] = TP[zl]

    def s2_copy(g, k):
        sl = Hb.at[g, :, x, c]
        return copy(sl, sl, s2s.at[g * 3 + k - 1], s2r.at[g * 3 + k - 1],
                    at_e(lax.rem(x + k, 4) * 2 + c))

    def s2_from(g, k):
        sl = Hb.at[g, :, lax.rem(x + 4 - k, 4), c]
        return copy(sl, sl, s2s.at[g * 3 + k - 1], s2r.at[g * 3 + k - 1], partner)

    def s3_copy(g):
        sl = Hb.at[g, :, :, c]
        return copy(sl, sl, s3s.at[g], s3r.at[g], sibling)

    def s3_from(g):
        sl = Hb.at[g, :, :, 1 - c]
        return copy(sl, sl, s3s.at[g], s3r.at[g], sibling)

    for g in (oh, h):
        def s1_wait(i):
            @pl.when(g * 8 + h * 4 + i != z)
            def _go():
                copy(hT, Hb.at[g, i, x, c], s1s.at[0], s1r.at[g * 4 + i], partner).wait_recv()

        loop(0, 4, s1_wait)
        for k in (1, 3, 2):
            s2_copy(g, k).start()

    w_pass(0)
    for g in (oh, h):
        for k in (1, 3, 2):
            s2_from(g, k).wait_recv()
        s3_copy(g).start()
    w_pass(1)
    s3_from(oh).wait_recv()

    def s_done(g):
        for k in (1, 2, 3):
            s2_copy(g, k).wait_send()
        s3_copy(g).wait_send()

    done.append(lambda: loop(0, 2, s_done))

    def z_copy(ch):
        return copy(Sb.at[ch], Rb.at[ch], zs_.at[ch], zr_.at[ch], partner)

    def rows_of(ch):
        return pl.ds(pl.multiple_of(ch * VC, 16), VC)

    def part(g, ch):
        tot = None
        for i in range(4):
            one = jnp.dot(Wc[i, rows_of(ch)], Hb[g, i].reshape(KS, TK), preferred_element_type=F32)
            tot = one if tot is None else tot + one
        return tot

    def chunk(ch):
        for k in (1, 3):
            f_from(ch, k).wait_recv()
        Sb[ch] = part(oh, ch)
        z_copy(ch).start()

        @pl.when(ch + 2 < NC)
        def _next():
            w_pass(ch + 2)

        @pl.when(ch == 0)
        def _feat():
            s3_from(h).wait_recv()

        L[ch] = part(h, ch)

    loop(0, NC, chunk)
    done.append(lambda: loop(0, NC, lambda ch: z_copy(ch).wait_send()))

    def ta_wait(k):
        frm = lax.rem(zl + 8 - k, 8)
        copy(TP.at[0], TQ.at[frm], tas.at[k - 1], tar.at[k - 1], partner).wait_recv()

    loop(1, 8, ta_wait)
    pick = jnp.logical_and(
        r_i // 16 == c_i % 8,
        jnp.logical_and((r_i // 2) % 8 == c_i // 16, r_i % 2 == (c_i // 8) % 2))
    TR[...] = permute(pick, TQ[...].reshape(TK, VP)).reshape(8, 16, VP)

    def tb_copy(k):
        to = lax.rem(e + k, 8)
        return copy(TR.at[to], TT.at[e], tbs.at[k - 1], tbr.at[k - 1], at_e(to))

    def tb_wait(k):
        frm = lax.rem(e + 8 - k, 8)
        copy(TR.at[0], TT.at[frm], tbs.at[k - 1], tbr.at[k - 1], sibling).wait_recv()

    loop(1, 8, lambda k: tb_copy(k).start())
    done.append(lambda: loop(1, 8, lambda k: tb_copy(k).wait_send()))
    TT[e] = TR[e]
    here = ids_ref[...] - v * VD
    lw = lw_ref[...]
    loop(1, 8, tb_wait)
    pick = jnp.logical_and(
        c_i // 16 == (r_i // 2) % 8,
        jnp.logical_and((c_i // 2) % 8 == r_i // 16, c_i % 2 == r_i % 2))
    TN[...] = lax.dot_general(
        TT[...].reshape(TK, VP), pick.astype(F32).astype(BF16), (((0,), (0,)), ((), ())),
        preferred_element_type=F32)

    lane = lax.broadcasted_iota(jnp.int32, (VC, TK), 0)
    low = F32(-3.0e38)

    def tea(ch):
        return TN[ch * VC:(ch + 1) * VC, :]

    m_s = jnp.full((1, TK), low, F32)
    m_t = jnp.full((1, TK), low, F32)
    for ch in range(NC):
        z_copy(ch).wait_recv()
        val = L[ch] + Rb[ch]
        L[ch] = val
        t = tea(ch)
        if ch == NC - 1:
            val = jnp.where(lane < TAIL, val, low)
            t = jnp.where(lane < TAIL, t, low)
        m_s = jnp.maximum(m_s, jnp.max(val, axis=0, keepdims=True))
        m_t = jnp.maximum(m_t, jnp.max(t, axis=0, keepdims=True))

    s_sum = jnp.zeros((1, TK), F32)
    s_gap = jnp.zeros((1, TK), F32)
    s_pick = jnp.zeros((1, TK), F32)
    s_tea = jnp.zeros((1, TK), F32)
    for ch in range(NC):
        val = L[ch]
        t = tea(ch)
        ex = jnp.exp(val - m_s)
        et = jnp.exp(t - m_t)
        eg = ex * (val - t)
        pk = jnp.where(lane + ch * VC == here, val, 0.0)
        if ch == NC - 1:
            ok = lane < TAIL
            ex = jnp.where(ok, ex, 0.0)
            et = jnp.where(ok, et, 0.0)
            eg = jnp.where(ok, eg, 0.0)
            pk = jnp.where(ok, pk, 0.0)
        s_sum = s_sum + jnp.sum(ex, axis=0, keepdims=True)
        s_gap = s_gap + jnp.sum(eg, axis=0, keepdims=True)
        s_pick = s_pick + jnp.sum(pk, axis=0, keepdims=True)
        s_tea = s_tea + jnp.sum(et, axis=0, keepdims=True)

    row = lax.broadcasted_iota(jnp.int32, (8, TK), 0)

    def stack(vals):
        acc = jnp.zeros((8, TK), F32)
        for n, val in enumerate(vals):
            acc = jnp.where(row == n, val, acc)
        return acc

    St[...] = stack((m_s, s_sum, s_gap, s_pick, m_t, s_tea))

    def combine(ref):
        ms = ref[0, 0:1]
        mt = ref[0, 4:5]
        for j in range(1, 8):
            ms = jnp.maximum(ms, ref[j, 0:1])
            mt = jnp.maximum(mt, ref[j, 4:5])
        a = b = p = t = jnp.zeros((1, TK), F32)
        for j in range(8):
            f = jnp.exp(ref[j, 0:1] - ms)
            a = a + ref[j, 1:2] * f
            b = b + ref[j, 2:3] * f
            p = p + ref[j, 3:4]
            t = t + ref[j, 5:6] * jnp.exp(ref[j, 4:5] - mt)
        return ms, a, b, p, mt, t

    def sa_copy(k):
        return copy(St, StA.at[e], sas.at[k - 1], sar.at[k - 1], at_e(lax.rem(e + k, 8)))

    def sa_wait(k):
        copy(St, StA.at[lax.rem(e + 8 - k, 8)], sas.at[k - 1], sar.at[k - 1], sibling).wait_recv()

    loop(1, 8, lambda k: sa_copy(k).start())
    done.append(lambda: loop(1, 8, lambda k: sa_copy(k).wait_send()))
    StA[e] = St[...]
    loop(1, 8, sa_wait)
    St2[...] = stack(combine(StA))

    def sb_copy(k):
        return copy(St2, StB.at[zl], sbs.at[k - 1], sbr.at[k - 1], at_z(h * 8 + lax.rem(zl + k, 8)))

    def sb_wait(k):
        copy(St2, StB.at[lax.rem(zl + 8 - k, 8)], sbs.at[k - 1], sbr.at[k - 1], sibling).wait_recv()

    loop(1, 8, lambda k: sb_copy(k).start())
    done.append(lambda: loop(1, 8, lambda k: sb_copy(k).wait_send()))
    StB[zl] = St2[...]
    loop(1, 8, sb_wait)
    ms, a, b, p, mt, t = combine(StB)
    s_lse = ms + jnp.log(a)
    t_lse = mt + jnp.log(t)
    div = b / a - s_lse + t_lse
    out_ref[OB:OB + 8, :] = stack((div, p - s_lse))

    def g_copy(ch):
        sl = GL.at[h, ch]
        return copy(sl, sl, gs.at[ch], gr.at[ch], partner)

    def g_wait(ch):
        sl = GL.at[oh, ch]
        copy(sl, sl, gs.at[ch], gr.at[ch], partner).wait_recv()

    for ch in range(NC):
        val = L[ch]
        gl = lw * jnp.exp(val - s_lse) * ((val - tea(ch)) - s_lse + t_lse - div)
        if ch == NC - 1:
            gl = jnp.where(lane < TAIL, gl, 0.0)
        GL[h, ch] = gl.astype(BF16)
        g_copy(ch).start()
    def c_copy(g, i):
        n = g * 4 + i
        return copy(GT.at[g, i, :, 1 - c], RC.at[g, i], cs.at[n], cr.at[n], sibling)

    def x_copy(g, i, k):
        to = lax.rem(x + k, 4)
        n = (g * 4 + i) * 3 + k - 1
        return copy(X1.at[g, i, to], RX.at[g, i, k - 1], xs.at[n], xr.at[n], at_e(to * 2 + c))

    def rq_copy(g, i):
        return copy(X2.at[g, i], RQ.at[g, ip], rqs.at[g * 4 + i], rqr.at[g * 4 + ip],
                    at_z(h * 8 + hb * 4 + i))

    def rz_copy(g):
        return copy(Qs.at[g], RZ.at[hb], rzs.at[g], rzr.at[hb], at_z(g * 8 + h * 4 + ip))

    def x_stage(g, i):
        c_copy(g, i).wait_recv()
        for xx in range(4):
            X1[g, i, xx] = GT[g, i, xx, c] + RC[g, i, xx]
        for k in (2, 1, 3):
            x_copy(g, i, k).start()

    def x_sum(g, i):
        for k in (1, 3, 2):
            x_copy(g, i, k).wait_recv()
        X2[g, i] = X1[g, i, x] + RX[g, i, 0] + RX[g, i, 1] + RX[g, i, 2]

    def not_me(i, fn):
        @pl.when(i != ip)
        def _go():
            fn()

    def q_stage(g, i):
        not_me(i, lambda: rq_copy(g, i).start())

        @pl.when(i == ip)
        def _own():
            RQ[g, ip] = X2[g, i]

    def z_stage(g):
        def q_wait(i):
            not_me(i, lambda: copy(
                X2.at[g, 0], RQ.at[g, i], rqs.at[0], rqr.at[g * 4 + i], partner).wait_recv())

        loop(0, 4, q_wait)
        Qs[g] = RQ[g, 0] + RQ[g, 1] + RQ[g, 2] + RQ[g, 3]
        dst = g * 8 + h * 4 + ip

        @pl.when(dst != z)
        def _go():
            rz_copy(g).start()

        @pl.when(dst == z)
        def _own():
            RZ[hb] = Qs[g]

    def mm(g, i, chs):
        tot = None
        for ch in chs:
            one = lax.dot_general(
                GL[g, ch], Wc[i, ch * VC:(ch + 1) * VC],
                (((0,), (0,)), ((), ())), preferred_element_type=F32)
            tot = one if tot is None else tot + one
        return tot

    def to_send(g, i, tot):
        GT[g, i] = tot.T.reshape(4, 2, OB, TK)
        c_copy(g, i).start()

    def own_mm(i):
        to_send(h, i, mm(h, i, range(NC)))

    loop(0, 4, own_mm)
    loop(0, 4, lambda i: x_stage(h, i))
    loop(0, 4, lambda i: x_sum(h, i))

    g_wait(0)
    g_wait(1)

    def oth_a(i):
        GA[i] = mm(oh, i, (0, 1))

    def oth_b(i):
        GA[i] = GA[i] + mm(oh, i, (2, 3))

    def oth_c(i):
        to_send(oh, i, GA[i] + mm(oh, i, (4,)))

    loop(0, 4, oth_a)
    g_wait(2)
    g_wait(3)
    loop(0, 4, oth_b)
    def cx_done(g, i):
        c_copy(g, i).wait_send()
        for k in (1, 2, 3):
            x_copy(g, i, k).wait_send()

    loop(0, 4, lambda i: cx_done(h, i))
    g_wait(4)

    def last(i):
        oth_c(i)


    loop(0, 4, lambda i: q_stage(h, i))
    loop(0, 4, last)
    loop(0, 4, lambda i: x_stage(oh, i))
    z_stage(h)

    def tail(i):
        x_sum(oh, i)
        q_stage(oh, i)

    loop(0, 4, tail)
    z_stage(oh)
    for fn in done:
        fn()
    loop(0, NC, lambda ch: g_copy(ch).wait_send())

    def q_done(i):
        cx_done(oh, i)
        for g in range(2):
            not_me(i, lambda: rq_copy(g, i).wait_send())

    loop(0, 4, q_done)

    def rz_wait(r):
        @pl.when(hb * 8 + r * 4 + ip != z)
        def _go():
            copy(Qs.at[0], RZ.at[r], rzs.at[0], rzr.at[r], partner).wait_recv()

    loop(0, 2, rz_wait)
    out_ref[0:OB, :] = RZ[0] + RZ[1]

    for g in range(2):
        @pl.when(g * 8 + h * 4 + ip != z)
        def _left():
            rz_copy(g).wait_send()


def split(both_ref, grad_ref, div_ref, slp_ref):
    grad_ref[...] = both_ref[0:OB, :]
    div_ref[...] = both_ref[OB:OB + 1, :]
    slp_ref[...] = both_ref[OB + 1:OB + 2, :]


def on_device(hidden, head_weight, teacher_logits, block_owner, sampled_ids, loss_weight):
    vm = pl.BlockSpec(memory_space=pltpu.VMEM)
    dma = pltpu.SemaphoreType.DMA
    both = pl.pallas_call(
        kernel,
        out_shape=jax.ShapeDtypeStruct((OB + 8, TK), F32),
        in_specs=[vm, vm, pl.BlockSpec(memory_space=pl.ANY), pl.BlockSpec(memory_space=pl.ANY), vm, vm],
        out_specs=vm,
        scratch_shapes=[
            pltpu.VMEM((VD, KS), BF16),
            pltpu.VMEM((2, 64 * VD), BF16),
            pltpu.VMEM((1, 128), jnp.int32),
            pltpu.VMEM((128, VP), F32),
            pltpu.VMEM((2, 4, 4, 2, OB, TK), BF16),
            pltpu.VMEM((4, VQ, KS), BF16),
            pltpu.VMEM((NC, VC, TK), F32),
            pltpu.VMEM((NC, VC, TK), F32),
            pltpu.VMEM((NC, VC, TK), F32),
            pltpu.VMEM((8, 16, VP), BF16),
            pltpu.VMEM((8, 16, VP), BF16),
            pltpu.VMEM((8, 16, VP), BF16),
            pltpu.VMEM((8, 16, VP), BF16),
            pltpu.VMEM((VP, TK), F32),
            pltpu.VMEM((8, TK), F32),
            pltpu.VMEM((8, 8, TK), F32),
            pltpu.VMEM((8, TK), F32),
            pltpu.VMEM((8, 8, TK), F32),
            pltpu.VMEM((4, TK, KS), F32),
            pltpu.VMEM((2, NC, VC, TK), BF16),
            pltpu.VMEM((2, 4, 4, 2, OB, TK), F32),
            pltpu.VMEM((2, 4, 4, OB, TK), F32),
            pltpu.VMEM((2, 4, 4, OB, TK), F32),
            pltpu.VMEM((2, 4, 3, OB, TK), F32),
            pltpu.VMEM((2, 4, OB, TK), F32),
            pltpu.VMEM((2, 4, OB, TK), F32),
            pltpu.VMEM((2, OB, TK), F32),
            pltpu.VMEM((2, OB, TK), F32),
            dma, dma,
            dma((8,)), dma((8,)),
            dma((6,)), dma((6,)),
            dma((2,)), dma((2,)),
            dma((2 * NC,)), dma((2 * NC,)),
            dma((2 * NC,)), dma((2 * NC,)),
            dma((NC,)), dma((NC,)),
            dma((7,)), dma((7,)),
            dma((7,)), dma((7,)),
            dma((7,)), dma((7,)),
            dma((7,)), dma((7,)),
            dma((NC,)), dma((NC,)),
            dma((8,)), dma((8,)),
            dma((24,)), dma((24,)),
            dma((8,)), dma((8,)),
            dma((2,)), dma((2,)),
        ],
        compiler_params=pltpu.CompilerParams(
            collective_id=0, has_side_effects=True, vmem_limit_bytes=56 * 2**20
        ),
    )(block_owner.reshape(1, 64), hidden.T, head_weight.T, teacher_logits,
      sampled_ids.reshape(1, TK), loss_weight.reshape(1, TK))
    grad, div, slp = pl.pallas_call(
        split,
        out_shape=[
            jax.ShapeDtypeStruct((OB, TK), F32),
            jax.ShapeDtypeStruct((1, TK), F32),
            jax.ShapeDtypeStruct((1, TK), F32),
        ],
        in_specs=[vm],
        out_specs=[vm, vm, vm],
    )(both)
    return grad.T, div.reshape(TK), slp.reshape(TK)


def solution(mesh):
    return jax.shard_map(
        on_device,
        mesh=mesh,
        in_specs=(
            P("dp", "vocab"),
            P("dp", "vocab"),
            P(("dp", "vocab"), None),
            P(),
            P("dp"),
            P("dp"),
        ),
        out_specs=(P("dp", "vocab"), P("dp"), P("dp")),
        check_vma=False,
    )
```

```python
import jax
import jax.numpy as jnp
from jax import lax
from jax.experimental import pallas as pl
from jax.experimental.pallas import tpu as pltpu
from jax.sharding import PartitionSpec as P

MESH = pl.DeviceIdType.MESH
F32 = jnp.float32
BF16 = jnp.bfloat16

VD = 1188
VC = 240
NC = 5
VQ = VC * NC
VP = 1280
TAIL = VD - (NC - 1) * VC
KS = 640
KH = 4 * KS
TK = 128
OB = 80
WIN = VP + 128


def kernel(
    own_ref, hT, w_ref, tea_ref, ids_ref, lw_ref,
    out_ref,
    Wv, Tv, Ow, TJ, Hb, Wc, Sb, Rb, L, TP, TQ, TR, TT, TN,
    St, StA, St2, StB, GA, GL, GT, RC, X1, RX, X2, RQ, Qs, RZ,
    lds, ldt, s1s, s1r, s2s, s2r, s3s, s3r, ws, wr, fs, fr, zs_, zr_,
    tas, tar, tbs, tbr, sas, sar, sbs, sbr, gs, gr, cs, cr, xs, xr, rqs, rqr, rzs, rzr,
):
    dp = lax.axis_index("dp")
    v = lax.axis_index("vocab")
    h = lax.div(dp, 4)
    q = lax.rem(dp, 4)
    zl = lax.div(v, 8)
    e = lax.rem(v, 8)
    x = lax.div(e, 2)
    c = lax.rem(e, 2)
    z = h * 8 + zl
    oh = 1 - h
    hb = lax.div(zl, 4)
    ip = lax.rem(zl, 4)
    done = []

    def at_z(zz):
        return (lax.div(zz, 8) * 4 + q, lax.rem(zz, 8) * 8 + e)

    def at_y(yy):
        return (h * 4 + yy, v)

    def at_e(ee):
        return (dp, zl * 8 + ee)

    partner = at_z(oh * 8 + zl)
    sibling = at_e(x * 2 + 1 - c)

    def copy(src, dst, ss, rs, dev):
        return pltpu.make_async_remote_copy(
            src_ref=src, dst_ref=dst, send_sem=ss, recv_sem=rs, device_id=dev, device_id_type=MESH
        )

    def loop(lo, hi, body):
        def step(k, carry):
            body(k)
            return carry
        lax.fori_loop(lo, hi, step, 0)

    load_w = pltpu.make_async_copy(w_ref, Wv, lds)
    load_w.start()
    load_t = pltpu.make_async_copy(tea_ref, Tv, ldt)
    load_t.start()
    barrier = pltpu.get_barrier_semaphore()

    def greet(dev):
        pl.semaphore_signal(barrier, inc=1, device_id=dev, device_id_type=MESH)

    loop(1, 16, lambda k: greet(at_z(lax.rem(z + k, 16))))
    loop(1, 4, lambda k: greet(at_y(lax.rem(q + k, 4))))
    loop(1, 8, lambda k: greet(at_e(lax.rem(e + k, 8))))

    pl.semaphore_wait(barrier, 25)

    def feat_copy(k):
        return copy(hT, Hb.at[h, ip, x, c], s1s.at[k], s1r.at[h * 4 + ip], at_z(hb * 8 + k))

    def not_self(k, fn):
        @pl.when(hb * 8 + k != z)
        def _go():
            fn(k)

    loop(0, 8, lambda k: not_self(k, lambda k: feat_copy(k).start()))
    done.append(lambda: loop(0, 8, lambda k: not_self(k, lambda k: feat_copy(k).wait_send())))

    @pl.when(hb == h)
    def _own():
        Hb[h, ip, x, c] = hT[...]

    load_w.wait()
    full = VD // 16 * 16
    Wc[q, 0:full] = Wv[0:full]
    last = Wv[full:VD].astype(F32)
    Wc[q, full:VQ] = jnp.concatenate([last, jnp.zeros((VQ - VD, KS), F32)], axis=0).astype(BF16)


    def w_part(ch, yy, lo, n):
        rows = pl.ds(pl.multiple_of(ch * VC + lo, 16), n)
        return Wc.at[lax.rem(yy, 4), rows]

    HALF = (0, 128), (128, VC - 128)

    def w_copy(ch, k):
        sl = w_part(ch, q, 0, VC)
        n = ch * 2 + k // 2
        return copy(sl, sl, ws.at[n], wr.at[n], at_y(lax.rem(q + k, 4)))

    def w_from(ch, k):
        sl = w_part(ch, q + 4 - k, 0, VC)
        n = ch * 2 + k // 2
        return copy(sl, sl, ws.at[n], wr.at[n], partner)

    def f_copy(ch, k):
        sl = w_part(ch, q + 4 - k, *HALF[k // 2])
        n = ch * 2 + k // 2
        return copy(sl, sl, fs.at[n], fr.at[n], at_y(lax.rem(q + k, 4)))

    def f_from(ch, k):
        sl = w_part(ch, q + 2, *HALF[k // 2])
        n = ch * 2 + k // 2
        return copy(sl, sl, fs.at[n], fr.at[n], partner)

    def w_send(ch):
        for k in (1, 3):
            w_copy(ch, k).start()

    def w_pass(ch):
        for k in (1, 3):
            w_from(ch, k).wait_recv()
            f_copy(ch, k).start()

        @pl.when(ch + 2 < NC)
        def _more():
            w_send(ch + 2)

    def w_done(ch):
        for k in (1, 3):
            w_copy(ch, k).wait_send()
            f_copy(ch, k).wait_send()

    w_send(0)
    w_send(1)
    done.append(lambda: loop(0, NC, w_done))

    load_t.wait()

    def unpack(j):
        s = j * VD
        a = pl.multiple_of(jnp.minimum(lax.div(s, 128) * 128, 64 * VD - WIN), 128)
        win = Tv[:, pl.ds(a, WIN)].astype(F32)
        win = pltpu.roll(win, WIN - (s - a), 1)
        TJ[pl.ds(j, 1), :] = win[0:1, 0:VP]
        TJ[pl.ds(64 + j, 1), :] = win[1:2, 0:VP]

    loop(0, 64, unpack)
    Ow[:, 0:64] = own_ref[...]
    Ow[:, 64:128] = own_ref[...]
    r_i = lax.broadcasted_iota(jnp.int32, (128, 128), 0)
    c_i = lax.broadcasted_iota(jnp.int32, (128, 128), 1)

    def permute(mask, rows):
        return jnp.dot(mask.astype(F32).astype(BF16), rows, preferred_element_type=F32).astype(BF16)

    block = (r_i // 16) * 8 + r_i % 8
    pick = jnp.logical_and((r_i // 8) % 2 == c_i // 64, Ow[...] == block)
    TP[...] = permute(pick, TJ[...].astype(BF16)).reshape(8, 16, VP)

    def ta_copy(k):
        to = lax.rem(zl + k, 8)
        return copy(TP.at[to], TQ.at[zl], tas.at[k - 1], tar.at[k - 1], at_z(h * 8 + to))

    loop(1, 8, lambda k: ta_copy(k).start())
    done.append(lambda: loop(1, 8, lambda k: ta_copy(k).wait_send()))
    TQ[zl] = TP[zl]

    def s2_copy(g, k):
        sl = Hb.at[g, :, x, c]
        return copy(sl, sl, s2s.at[g * 3 + k - 1], s2r.at[g * 3 + k - 1],
                    at_e(lax.rem(x + k, 4) * 2 + c))

    def s2_from(g, k):
        sl = Hb.at[g, :, lax.rem(x + 4 - k, 4), c]
        return copy(sl, sl, s2s.at[g * 3 + k - 1], s2r.at[g * 3 + k - 1], partner)

    def s3_copy(g):
        sl = Hb.at[g, :, :, c]
        return copy(sl, sl, s3s.at[g], s3r.at[g], sibling)

    def s3_from(g):
        sl = Hb.at[g, :, :, 1 - c]
        return copy(sl, sl, s3s.at[g], s3r.at[g], sibling)

    for g in (oh, h):
        def s1_wait(i):
            @pl.when(g * 8 + h * 4 + i != z)
            def _go():
                copy(hT, Hb.at[g, i, x, c], s1s.at[0], s1r.at[g * 4 + i], partner).wait_recv()

        loop(0, 4, s1_wait)
        for k in (1, 3, 2):
            s2_copy(g, k).start()

    w_pass(0)
    for g in (oh, h):
        for k in (1, 3, 2):
            s2_from(g, k).wait_recv()
        s3_copy(g).start()
    w_pass(1)
    s3_from(oh).wait_recv()

    def s_done(g):
        for k in (1, 2, 3):
            s2_copy(g, k).wait_send()
        s3_copy(g).wait_send()

    done.append(lambda: loop(0, 2, s_done))

    def z_copy(ch):
        return copy(Sb.at[ch], Rb.at[ch], zs_.at[ch], zr_.at[ch], partner)

    def rows_of(ch):
        return pl.ds(pl.multiple_of(ch * VC, 16), VC)

    def part(g, ch):
        tot = None
        for i in range(4):
            one = jnp.dot(Wc[i, rows_of(ch)], Hb[g, i].reshape(KS, TK), preferred_element_type=F32)
            tot = one if tot is None else tot + one
        return tot

    def chunk(ch):
        for k in (1, 3):
            f_from(ch, k).wait_recv()
        Sb[ch] = part(oh, ch)
        z_copy(ch).start()

        @pl.when(ch + 2 < NC)
        def _next():
            w_pass(ch + 2)

        @pl.when(ch == 0)
        def _feat():
            s3_from(h).wait_recv()

        L[ch] = part(h, ch)

    loop(0, NC, chunk)
    done.append(lambda: loop(0, NC, lambda ch: z_copy(ch).wait_send()))

    def ta_wait(k):
        frm = lax.rem(zl + 8 - k, 8)
        copy(TP.at[0], TQ.at[frm], tas.at[k - 1], tar.at[k - 1], partner).wait_recv()

    loop(1, 8, ta_wait)
    pick = jnp.logical_and(
        r_i // 16 == c_i % 8,
        jnp.logical_and((r_i // 2) % 8 == c_i // 16, r_i % 2 == (c_i // 8) % 2))
    TR[...] = permute(pick, TQ[...].reshape(TK, VP)).reshape(8, 16, VP)

    def tb_copy(k):
        to = lax.rem(e + k, 8)
        return copy(TR.at[to], TT.at[e], tbs.at[k - 1], tbr.at[k - 1], at_e(to))

    def tb_wait(k):
        frm = lax.rem(e + 8 - k, 8)
        copy(TR.at[0], TT.at[frm], tbs.at[k - 1], tbr.at[k - 1], sibling).wait_recv()

    loop(1, 8, lambda k: tb_copy(k).start())
    done.append(lambda: loop(1, 8, lambda k: tb_copy(k).wait_send()))
    TT[e] = TR[e]
    here = ids_ref[...] - v * VD
    lw = lw_ref[...]
    loop(1, 8, tb_wait)
    pick = jnp.logical_and(
        c_i // 16 == (r_i // 2) % 8,
        jnp.logical_and((c_i // 2) % 8 == r_i // 16, c_i % 2 == r_i % 2))
    TN[...] = lax.dot_general(
        TT[...].reshape(TK, VP), pick.astype(F32).astype(BF16), (((0,), (0,)), ((), ())),
        preferred_element_type=F32)

    lane = lax.broadcasted_iota(jnp.int32, (VC, TK), 0)
    low = F32(-3.0e38)

    def tea(ch):
        return TN[ch * VC:(ch + 1) * VC, :]

    m_s = jnp.full((1, TK), low, F32)
    m_t = jnp.full((1, TK), low, F32)
    for ch in range(NC):
        t = tea(ch)
        if ch == NC - 1:
            t = jnp.where(lane < TAIL, t, low)
        m_t = jnp.maximum(m_t, jnp.max(t, axis=0, keepdims=True))
    s_tea = jnp.zeros((1, TK), F32)
    for ch in range(NC):
        et = jnp.exp(tea(ch) - m_t)
        if ch == NC - 1:
            et = jnp.where(lane < TAIL, et, 0.0)
        s_tea = s_tea + jnp.sum(et, axis=0, keepdims=True)

    for ch in range(NC):
        z_copy(ch).wait_recv()
        val = L[ch] + Rb[ch]
        L[ch] = val
        if ch == NC - 1:
            val = jnp.where(lane < TAIL, val, low)
        m_s = jnp.maximum(m_s, jnp.max(val, axis=0, keepdims=True))

    s_sum = jnp.zeros((1, TK), F32)
    s_gap = jnp.zeros((1, TK), F32)
    s_pick = jnp.zeros((1, TK), F32)
    for ch in range(NC):
        val = L[ch]
        t = tea(ch)
        ex = jnp.exp(val - m_s)
        eg = ex * (val - t)
        pk = jnp.where(lane + ch * VC == here, val, 0.0)
        if ch == NC - 1:
            ok = lane < TAIL
            ex = jnp.where(ok, ex, 0.0)
            eg = jnp.where(ok, eg, 0.0)
            pk = jnp.where(ok, pk, 0.0)
        s_sum = s_sum + jnp.sum(ex, axis=0, keepdims=True)
        s_gap = s_gap + jnp.sum(eg, axis=0, keepdims=True)
        s_pick = s_pick + jnp.sum(pk, axis=0, keepdims=True)

    row = lax.broadcasted_iota(jnp.int32, (8, TK), 0)

    def stack(vals):
        acc = jnp.zeros((8, TK), F32)
        for n, val in enumerate(vals):
            acc = jnp.where(row == n, val, acc)
        return acc

    St[...] = stack((m_s, s_sum, s_gap, s_pick, m_t, s_tea))

    def combine(ref):
        ms = ref[0, 0:1]
        mt = ref[0, 4:5]
        for j in range(1, 8):
            ms = jnp.maximum(ms, ref[j, 0:1])
            mt = jnp.maximum(mt, ref[j, 4:5])
        a = b = p = t = jnp.zeros((1, TK), F32)
        for j in range(8):
            f = jnp.exp(ref[j, 0:1] - ms)
            a = a + ref[j, 1:2] * f
            b = b + ref[j, 2:3] * f
            p = p + ref[j, 3:4]
            t = t + ref[j, 5:6] * jnp.exp(ref[j, 4:5] - mt)
        return ms, a, b, p, mt, t

    def sa_copy(k):
        return copy(St, StA.at[e], sas.at[k - 1], sar.at[k - 1], at_e(lax.rem(e + k, 8)))

    def sa_wait(k):
        copy(St, StA.at[lax.rem(e + 8 - k, 8)], sas.at[k - 1], sar.at[k - 1], sibling).wait_recv()

    loop(1, 8, lambda k: sa_copy(k).start())
    done.append(lambda: loop(1, 8, lambda k: sa_copy(k).wait_send()))
    StA[e] = St[...]
    loop(1, 8, sa_wait)
    St2[...] = stack(combine(StA))

    def sb_copy(k):
        return copy(St2, StB.at[zl], sbs.at[k - 1], sbr.at[k - 1], at_z(h * 8 + lax.rem(zl + k, 8)))

    def sb_wait(k):
        copy(St2, StB.at[lax.rem(zl + 8 - k, 8)], sbs.at[k - 1], sbr.at[k - 1], sibling).wait_recv()

    loop(1, 8, lambda k: sb_copy(k).start())
    done.append(lambda: loop(1, 8, lambda k: sb_copy(k).wait_send()))
    StB[zl] = St2[...]
    loop(1, 8, sb_wait)
    ms, a, b, p, mt, t = combine(StB)
    s_lse = ms + jnp.log(a)
    t_lse = mt + jnp.log(t)
    div = b / a - s_lse + t_lse
    out_ref[OB:OB + 8, :] = stack((div, p - s_lse))

    def g_copy(ch):
        sl = GL.at[h, ch]
        return copy(sl, sl, gs.at[ch], gr.at[ch], partner)

    def g_wait(ch):
        sl = GL.at[oh, ch]
        copy(sl, sl, gs.at[ch], gr.at[ch], partner).wait_recv()

    for ch in range(NC):
        val = L[ch]
        gl = lw * jnp.exp(val - s_lse) * ((val - tea(ch)) - s_lse + t_lse - div)
        if ch == NC - 1:
            gl = jnp.where(lane < TAIL, gl, 0.0)
        GL[h, ch] = gl.astype(BF16)
        g_copy(ch).start()
    def c_copy(g, i):
        n = g * 4 + i
        return copy(GT.at[g, i, :, 1 - c], RC.at[g, i], cs.at[n], cr.at[n], sibling)

    def x_copy(g, i, k):
        to = lax.rem(x + k, 4)
        n = (g * 4 + i) * 3 + k - 1
        return copy(X1.at[g, i, to], RX.at[g, i, k - 1], xs.at[n], xr.at[n], at_e(to * 2 + c))

    def rq_copy(g, i):
        return copy(X2.at[g, i], RQ.at[g, ip], rqs.at[g * 4 + i], rqr.at[g * 4 + ip],
                    at_z(h * 8 + hb * 4 + i))

    def rz_copy(g):
        return copy(Qs.at[g], RZ.at[hb], rzs.at[g], rzr.at[hb], at_z(g * 8 + h * 4 + ip))

    def x_stage(g, i):
        c_copy(g, i).wait_recv()
        for xx in range(4):
            X1[g, i, xx] = GT[g, i, xx, c] + RC[g, i, xx]
        for k in (2, 1, 3):
            x_copy(g, i, k).start()

    def x_sum(g, i):
        for k in (1, 3, 2):
            x_copy(g, i, k).wait_recv()
        X2[g, i] = X1[g, i, x] + RX[g, i, 0] + RX[g, i, 1] + RX[g, i, 2]

    def not_me(i, fn):
        @pl.when(i != ip)
        def _go():
            fn()

    def q_stage(g, i):
        not_me(i, lambda: rq_copy(g, i).start())

        @pl.when(i == ip)
        def _own():
            RQ[g, ip] = X2[g, i]

    def z_stage(g):
        def q_wait(i):
            not_me(i, lambda: copy(
                X2.at[g, 0], RQ.at[g, i], rqs.at[0], rqr.at[g * 4 + i], partner).wait_recv())

        loop(0, 4, q_wait)
        Qs[g] = RQ[g, 0] + RQ[g, 1] + RQ[g, 2] + RQ[g, 3]
        dst = g * 8 + h * 4 + ip

        @pl.when(dst != z)
        def _go():
            rz_copy(g).start()

        @pl.when(dst == z)
        def _own():
            RZ[hb] = Qs[g]

    def mm(g, i, chs):
        tot = None
        for ch in chs:
            one = lax.dot_general(
                GL[g, ch], Wc[i, ch * VC:(ch + 1) * VC],
                (((0,), (0,)), ((), ())), preferred_element_type=F32)
            tot = one if tot is None else tot + one
        return tot

    def to_send(g, i, tot):
        GT[g, i] = tot.T.reshape(4, 2, OB, TK)
        c_copy(g, i).start()

    def own_mm(i):
        to_send(h, i, mm(h, i, range(NC)))

    loop(0, 4, own_mm)
    loop(0, 4, lambda i: x_stage(h, i))
    loop(0, 4, lambda i: x_sum(h, i))

    g_wait(0)
    g_wait(1)

    def oth_a(i):
        GA[i] = mm(oh, i, (0, 1))

    def oth_b(i):
        GA[i] = GA[i] + mm(oh, i, (2, 3))

    def oth_c(i):
        to_send(oh, i, GA[i] + mm(oh, i, (4,)))

    loop(0, 4, oth_a)
    g_wait(2)
    g_wait(3)
    loop(0, 4, oth_b)
    def cx_done(g, i):
        c_copy(g, i).wait_send()
        for k in (1, 2, 3):
            x_copy(g, i, k).wait_send()

    loop(0, 4, lambda i: cx_done(h, i))
    g_wait(4)

    def last(i):
        oth_c(i)


    loop(0, 4, lambda i: q_stage(h, i))
    loop(0, 4, last)
    loop(0, 4, lambda i: x_stage(oh, i))
    z_stage(h)

    def tail(i):
        x_sum(oh, i)
        q_stage(oh, i)

    loop(0, 4, tail)
    z_stage(oh)
    for fn in done:
        fn()
    loop(0, NC, lambda ch: g_copy(ch).wait_send())

    def q_done(i):
        cx_done(oh, i)
        for g in range(2):
            not_me(i, lambda: rq_copy(g, i).wait_send())

    loop(0, 4, q_done)

    def rz_wait(r):
        @pl.when(hb * 8 + r * 4 + ip != z)
        def _go():
            copy(Qs.at[0], RZ.at[r], rzs.at[0], rzr.at[r], partner).wait_recv()

    loop(0, 2, rz_wait)
    out_ref[0:OB, :] = RZ[0] + RZ[1]

    for g in range(2):
        @pl.when(g * 8 + h * 4 + ip != z)
        def _left():
            rz_copy(g).wait_send()


def split(both_ref, grad_ref, div_ref, slp_ref):
    grad_ref[...] = both_ref[0:OB, :]
    div_ref[...] = both_ref[OB:OB + 1, :]
    slp_ref[...] = both_ref[OB + 1:OB + 2, :]


def on_device(hidden, head_weight, teacher_logits, block_owner, sampled_ids, loss_weight):
    vm = pl.BlockSpec(memory_space=pltpu.VMEM)
    dma = pltpu.SemaphoreType.DMA
    both = pl.pallas_call(
        kernel,
        out_shape=jax.ShapeDtypeStruct((OB + 8, TK), F32),
        in_specs=[vm, vm, pl.BlockSpec(memory_space=pl.ANY), pl.BlockSpec(memory_space=pl.ANY), vm, vm],
        out_specs=vm,
        scratch_shapes=[
            pltpu.VMEM((VD, KS), BF16),
            pltpu.VMEM((2, 64 * VD), BF16),
            pltpu.VMEM((1, 128), jnp.int32),
            pltpu.VMEM((128, VP), F32),
            pltpu.VMEM((2, 4, 4, 2, OB, TK), BF16),
            pltpu.VMEM((4, VQ, KS), BF16),
            pltpu.VMEM((NC, VC, TK), F32),
            pltpu.VMEM((NC, VC, TK), F32),
            pltpu.VMEM((NC, VC, TK), F32),
            pltpu.VMEM((8, 16, VP), BF16),
            pltpu.VMEM((8, 16, VP), BF16),
            pltpu.VMEM((8, 16, VP), BF16),
            pltpu.VMEM((8, 16, VP), BF16),
            pltpu.VMEM((VP, TK), F32),
            pltpu.VMEM((8, TK), F32),
            pltpu.VMEM((8, 8, TK), F32),
            pltpu.VMEM((8, TK), F32),
            pltpu.VMEM((8, 8, TK), F32),
            pltpu.VMEM((4, TK, KS), F32),
            pltpu.VMEM((2, NC, VC, TK), BF16),
            pltpu.VMEM((2, 4, 4, 2, OB, TK), F32),
            pltpu.VMEM((2, 4, 4, OB, TK), F32),
            pltpu.VMEM((2, 4, 4, OB, TK), F32),
            pltpu.VMEM((2, 4, 3, OB, TK), F32),
            pltpu.VMEM((2, 4, OB, TK), F32),
            pltpu.VMEM((2, 4, OB, TK), F32),
            pltpu.VMEM((2, OB, TK), F32),
            pltpu.VMEM((2, OB, TK), F32),
            dma, dma,
            dma((8,)), dma((8,)),
            dma((6,)), dma((6,)),
            dma((2,)), dma((2,)),
            dma((2 * NC,)), dma((2 * NC,)),
            dma((2 * NC,)), dma((2 * NC,)),
            dma((NC,)), dma((NC,)),
            dma((7,)), dma((7,)),
            dma((7,)), dma((7,)),
            dma((7,)), dma((7,)),
            dma((7,)), dma((7,)),
            dma((NC,)), dma((NC,)),
            dma((8,)), dma((8,)),
            dma((24,)), dma((24,)),
            dma((8,)), dma((8,)),
            dma((2,)), dma((2,)),
        ],
        compiler_params=pltpu.CompilerParams(
            collective_id=0, has_side_effects=True, vmem_limit_bytes=56 * 2**20
        ),
    )(block_owner.reshape(1, 64), hidden.T, head_weight.T, teacher_logits,
      sampled_ids.reshape(1, TK), loss_weight.reshape(1, TK))
    grad, div, slp = pl.pallas_call(
        split,
        out_shape=[
            jax.ShapeDtypeStruct((OB, TK), F32),
            jax.ShapeDtypeStruct((1, TK), F32),
            jax.ShapeDtypeStruct((1, TK), F32),
        ],
        in_specs=[vm],
        out_specs=[vm, vm, vm],
    )(both)
    return grad.T, div.reshape(TK), slp.reshape(TK)


def solution(mesh):
    return jax.shard_map(
        on_device,
        mesh=mesh,
        in_specs=(
            P("dp", "vocab"),
            P("dp", "vocab"),
            P(("dp", "vocab"), None),
            P(),
            P("dp"),
            P("dp"),
        ),
        out_specs=(P("dp", "vocab"), P("dp"), P("dp")),
        check_vma=False,
    )
```
